256 devices in a mesh: row: 64 (over x, y, z_hi, core), rep: 4 (over z_lo).
Axes of the slice: x: 4, y: 4, z: 8 (z_hi: 2, z_lo: 4; z = z_hi * 4 + z_lo), core: 2. Of those that a mesh axis runs over, the one named last changes fastest.
Arguments:
- features: float32 [32768, 128], P(('row', 'rep')), may hold values from -6 to 6
- tiles: float32 [256, 4, 8, 128, 128], P('row', 'rep'), may hold values from -0.15625 to 0.15625
- columns: int32 [256, 4, 8], P('row', 'rep'), may hold values from 0 to 63, as said below
- counts: int32 [256, 4], P('row', 'rep'), may hold values from 1 to 8, as said below
- self_one: float32 [128, 256], replicated, may hold values from -0.5 to 0.5
- neigh_one: float32 [128, 256], replicated, may hold values from -0.5 to 0.5
- bias_one: float32 [256], replicated, may hold values from -3 to 3
- self_two: float32 [256, 172], replicated, may hold values from -0.375 to 0.375
- neigh_two: float32 [256, 172], replicated, may hold values from -0.375 to 0.375
- bias_two: float32 [172], replicated, may hold values from -3 to 3
- cotangent: float32 [32768, 172], P(('row', 'rep')), may hold values from -0.03314563 to 0.03314563
Outputs:
- logits: float32 [32768, 172], P(('row', 'rep'))
- grad_self_one: float32 [128, 256], replicated
- grad_neigh_one: float32 [128, 256], replicated
- grad_bias_one: float32 [256], replicated
- grad_self_two: float32 [256, 172], replicated
- grad_neigh_two: float32 [256, 172], replicated
- grad_bias_two: float32 [172], replicated
The draws below stay inside these ranges and needn't reach their ends.
Inputs may be any that keep to these rules, and one draw needn't show every extreme that they name: `columns`: in each list the first 8 entries are distinct, and entry 0 of the lists of row block b is b // 4; only the first counts[b, j] entries are live. `counts`: A few groups of 4 consecutive row blocks hold far more live tiles than the others; 8 is reached in every draw.
All inputs are finite; a program needn't handle non-finite values.
Results may differ from the reference program's by a relative error of at most 0.0003.
Values sent between devices are 32-bit elements; how exact they have to be, the bound alone decides.
No kernel may reach another device: no remote copies, remote signals or barrier semaphores. Data moves between devices by JAX's collectives and lax.ppermute only.
A program may use at most 64 MiB of HBM per device.

```python
import jax
import jax.numpy as jnp
from jax import lax

BLK = 128
D_IN = 128
HID = 256
CLS = 172
KT = 8
NB = 256
NODES = 32768
N_ROW = 64
N_REP = 4


def draw_columns(key, part):
    key = jax.random.fold_in(key, 11)
    lists = N_ROW * N_REP * N_REP
    keys = jax.random.split(key, lists)
    offsets = jax.vmap(lambda single: jax.random.permutation(single, N_ROW - 1))(keys)[:, :KT - 1] + 1
    offsets = jnp.concatenate([jnp.zeros((lists, 1), jnp.int32), offsets.astype(jnp.int32)], axis=1)
    owners = jnp.arange(lists, dtype=jnp.int32) // (N_REP * N_REP)
    picked = (owners[:, None] + offsets) % N_ROW
    return picked.reshape(N_ROW * N_REP, N_REP, KT).astype(jnp.int32)


def draw_counts(key, part):
    key = jax.random.fold_in(key, 23)
    keys = jax.random.split(key, 6)
    base = jax.random.randint(keys[0], (N_ROW * N_REP, N_REP), 1, 4)
    heavy = jax.random.randint(keys[1], (N_ROW,), 0, 8) == 0
    chosen = jax.random.randint(keys[2], (), 0, N_ROW)
    heavy = heavy | (jnp.arange(N_ROW, dtype=jnp.int32) == chosen)
    heavy_vals = jax.random.randint(keys[3], (N_ROW * N_REP, N_REP), KT // 2 + 1, KT + 1)
    heavy_rows = jnp.repeat(heavy, N_REP)[:, None]
    result = jnp.where(heavy_rows, heavy_vals, base)
    block_pick = jax.random.randint(keys[4], (), 0, N_REP)
    layer_pick = jax.random.randint(keys[5], (), 0, N_REP)
    result = result.at[chosen * N_REP + block_pick, layer_pick].set(KT)
    return result.astype(jnp.int32)


def steps_of(stream_key, extent, cuts, least, high):
    def one(position, blocks):
        heights = jax.random.uniform(jax.random.fold_in(jax.random.fold_in(stream_key, 6), position), (blocks,), jnp.float32, least / len(cuts), high / len(cuts))
        return jnp.repeat(jnp.exp(heights), extent[position] // blocks).reshape((-1,) + (1,) * (len(extent) - position - 1))

    level = one(*cuts[0])
    for cut in cuts[1:]:
        level = level * one(*cut)
    return level


def bell_draw(stream_key, shape, scale, limit, cuts=(), held_as=jnp.bfloat16):
    array = jax.random.normal(stream_key, shape, jnp.float32) * scale
    if len(cuts) > 0:
        array = steps_of(stream_key, shape, cuts, -0.22, 0.18) * array
    return jnp.clip(array, min=-limit, max=limit).astype(held_as)


def setup_inputs(seed: int = 0) -> dict:
    arg_keys = jax.random.split(jax.random.key(seed), 12)
    features = bell_draw(arg_keys[0], (NODES, D_IN), 1.0, 6.0, ((0, 256),), jnp.float32)
    tiles = bell_draw(arg_keys[1], (NB, N_REP, KT, BLK, BLK), (10 * BLK) ** -0.5, 0.15625, ((0, 64), (1, 4)), jnp.float32)
    columns = draw_columns(jax.random.fold_in(arg_keys[11], 71), 0)
    counts = draw_counts(jax.random.fold_in(arg_keys[11], 71), 0)
    self_one = bell_draw(arg_keys[4], (D_IN, HID), D_IN ** -0.5, 0.5, (), jnp.float32)
    neigh_one = bell_draw(arg_keys[5], (D_IN, HID), D_IN ** -0.5, 0.5, (), jnp.float32)
    bias_one = bell_draw(arg_keys[6], (HID,), 0.5, 3.0, (), jnp.float32)
    self_two = bell_draw(arg_keys[7], (HID, CLS), HID ** -0.5, 0.375, (), jnp.float32)
    neigh_two = bell_draw(arg_keys[8], (HID, CLS), HID ** -0.5, 0.375, (), jnp.float32)
    bias_two = bell_draw(arg_keys[9], (CLS,), 0.5, 3.0, (), jnp.float32)
    cotangent = bell_draw(arg_keys[10], (NODES, CLS), (NODES ** -0.5), 0.03314563, ((0, 256),), jnp.float32)
    return dict(features=features, tiles=tiles, columns=columns, counts=counts, self_one=self_one, neigh_one=neigh_one, bias_one=bias_one, self_two=self_two, neigh_two=neigh_two, bias_two=bias_two, cotangent=cotangent)


def aggregate(tiles, columns, counts, source):
    width = source.shape[1]
    blocks = source.reshape(source.shape[0] // BLK, BLK, width)
    rep_ids = jnp.arange(N_REP, dtype=jnp.int32)
    slots = jnp.arange(KT, dtype=jnp.int32)

    def one_row(items):
        tile_row, col_row, count_row = items
        global_cols = (col_row * N_REP + rep_ids[:, None]).astype(jnp.int32)
        picked = blocks[global_cols]
        keep = (slots[None, :] < count_row[:, None]).astype(source.dtype)
        return jnp.einsum('jkab,jkbw,jk->aw', tile_row, picked, keep, precision=lax.Precision.HIGHEST)
    summed = lax.map(one_row, (tiles, columns, counts))
    return summed.reshape(-1, width)

def reference(features, tiles, columns, counts, self_one, neigh_one, bias_one, self_two, neigh_two, bias_two, cotangent):
    highest = lax.Precision.HIGHEST

    def forward(s_one, n_one, b_one, s_two, n_two, b_two):
        agg_one = aggregate(tiles, columns, counts, features)
        pre_one = jnp.dot(features, s_one, precision=highest) + jnp.dot(agg_one, n_one, precision=highest) + b_one
        hidden = jax.nn.silu(pre_one)
        agg_two = aggregate(tiles, columns, counts, hidden)
        return jnp.dot(hidden, s_two, precision=highest) + jnp.dot(agg_two, n_two, precision=highest) + b_two
    logits, pull = jax.vjp(forward, self_one, neigh_one, bias_one, self_two, neigh_two, bias_two)
    grads = pull(cotangent)
    return (logits, grads[0], grads[1], grads[2], grads[3], grads[4], grads[5])
```

```python
import jax
import jax.numpy as jnp
from jax import lax
from jax.experimental import pallas as pl
from jax.experimental.pallas import tpu as pltpu
from jax.sharding import PartitionSpec as P

NX, NY, NZ, NC, NR = 4, 4, 2, 2, 4
SIDE = 128
CLS = 172
CP = 176
HP = CP // 2
GROWS = 1280
F32 = jnp.float32
VMEM = pl.BlockSpec(memory_space=pltpu.VMEM)
SMEM = pl.BlockSpec(memory_space=pltpu.SMEM)
ANY = pl.BlockSpec(memory_space=pl.ANY)
PARAMS = pltpu.CompilerParams(vmem_limit_bytes=24 * 1024 * 1024)


def row_perm(dx=0, dy=0, dz=0, dc=0):
    pairs = []
    for x in range(NX):
        for y in range(NY):
            for z in range(NZ):
                for c in range(NC):
                    src = ((x * NY + y) * NZ + z) * NC + c
                    dst = (((x + dx) % NX * NY + (y + dy) % NY) * NZ + (z ^ dz)) * NC + (c ^ dc)
                    pairs.append((src, dst))
    return pairs


def send(a, dx=0, dy=0, dz=0, dc=0):
    return lax.ppermute(a, "row", row_perm(dx, dy, dz, dc))


def send_rep(a, d):
    return lax.ppermute(a, "rep", [(j, (j + d) % NR) for j in range(NR)])


def shift(first, d):
    return {"dx": d} if first else {"dy": d}


def split(a):
    hi = a.astype(jnp.bfloat16)
    lo = (a - hi.astype(F32)).astype(jnp.bfloat16)
    return hi, lo


def dot3(a, b, dims=((1,), (0,))):
    dn = (dims, ((), ()))
    ah, al = split(a)
    bh, bl = split(b)
    mm = lambda p, q: lax.dot_general(p, q, dn, preferred_element_type=F32)
    return mm(ah, bh) + (mm(ah, bl) + mm(al, bh))


def relative(c, me):
    diff = c ^ me
    dc = diff & 1
    dz = (diff >> 1) & 1
    dy = ((c >> 2) - (me >> 2)) & 3
    dx = ((c >> 4) - (me >> 4)) & 3
    return dx, dy, dz, dc


def load_pieces(refs, bufs, sems):
    copies = []
    for h in range(2):
        for k in range(8):
            copies.append(
                pltpu.make_async_copy(
                    refs[h * 8 + k], bufs[h].at[pl.ds(k * 8, 8)], sems.at[h * 8 + k]
                )
            )
    for c in copies:
        c.start()
    for c in copies:
        c.wait()


def piece_index(c, me):
    dx, dy, dz, dc = relative(c, me)
    return ((dc * 4 + dy) * 4 + dx) * 2 + dz, ((dc * 4 + dx) * 4 + dy) * 2 + dz


def agg_one_kernel(place, columns, counts, tiles, *rest):
    refs, outs, (buf0, buf1, sems) = rest[:16], rest[16:20], rest[20:]
    me, rep = place[0], place[1]
    load_pieces(refs, (buf0, buf1), sems)
    for d in range(NR):
        block = (rep + d) & 3

        def step(s, acc, block=block):
            i0, i1 = piece_index(columns[block, s], me)
            piece = jnp.concatenate([buf0[i0], buf1[i1]], axis=0)
            return acc + dot3(tiles[block, 0, s], piece)

        outs[d][...] = lax.fori_loop(0, counts[block], step, jnp.zeros((SIDE, SIDE), F32))


def agg_two_kernel(place, columns, counts, tiles, *rest):
    refs, outs, (buf0, buf1, sems) = rest[:16], rest[16:20], rest[20:]
    me, rep = place[0], place[1]
    load_pieces(refs, (buf0, buf1), sems)
    for d in range(NR):
        block = (rep + d) & 3

        def step(s, acc, block=block):
            i0, i1 = piece_index(columns[block, s], me)
            piece = jnp.concatenate([buf0[i0], buf1[i1]], axis=0)
            return acc + dot3(piece, tiles[block, 0, s], ((1,), (1,)))

        outs[d][...] = lax.fori_loop(0, counts[block], step, jnp.zeros((CP, SIDE), F32))


def transposed_kernel(place, columns, counts, tiles, ct0, ct1, ct2, ct3, own0, own1, oth0, oth1):
    me, rep = place[0], place[1]
    for o in (own0, own1, oth0, oth1):
        o[...] = jnp.zeros(o.shape, F32)
    for d, ct in enumerate((ct0, ct1, ct2, ct3)):
        block = (rep + d) & 3

        def step(s, _, block=block, ct=ct):
            dx, dy, dz, dc = relative(columns[block, s], me)
            i0 = (dx * 4 + dy) * 2 + dz
            i1 = (dy * 4 + dx) * 2 + dz
            r = dot3(ct[...], tiles[block, 0, s])

            @pl.when(dc == 0)
            def _():
                own0[i0] += r[:HP]
                own1[i1] += r[HP:]

            @pl.when(dc != 0)
            def _():
                oth0[i0] += r[:HP]
                oth1[i1] += r[HP:]

            return 0

        lax.fori_loop(0, counts[block], step, 0)


def transpose_kernel(cot, out):
    out[pl.ds(CP - 8, 8)] = jnp.zeros((8, SIDE), F32)
    out[pl.ds(0, CLS)] = cot[...].T


def hidden_kernel(a0, a1, a2, a3, feat, self_one, neigh_one, bias, neigh_two, agg, pre, yt):
    total = (a0[...] + a1[...]) + (a2[...] + a3[...])
    agg[...] = total
    p = dot3(feat[...], self_one[...]) + dot3(total, neigh_one[...]) + bias[...]
    pre[...] = p
    h = p * jax.nn.sigmoid(p)
    y = dot3(neigh_two[...].T, h, ((1,), (1,)))
    yt[pl.ds(CP - 8, 8)] = jnp.zeros((8, SIDE), F32)
    yt[pl.ds(0, CLS)] = y


def grad_kernel(place, g0, g1, gz, pre, agg, feat, cot, ct, self_two, neigh_two, bias_two,
                base, same, other, packed):
    me = place[0]
    p = pre[...]
    s = jax.nn.sigmoid(p)
    h = p * s
    base[...] = dot3(h, self_two[...]) + bias_two[...]
    gt = jnp.concatenate([g0[...], g1[...]], axis=0) + gz[...]
    gn = gt.T[:, :CLS]
    gh = dot3(cot[...], self_two[...], ((1,), (1,))) + dot3(gn, neigh_two[...], ((1,), (1,)))
    gp = gh * s * (1.0 + p * (1.0 - s))
    bias_one_grad = jnp.sum(gp, axis=0, keepdims=True)
    bias_two_grad = jnp.sum(cot[...], axis=0, keepdims=True)

    def put(start, value):
        rows = value.shape[0]
        packed[pl.ds(start, rows)] = value[:, :SIDE]
        packed[pl.ds(608 + start, rows)] = value[:, SIDE:]

    packed[pl.ds(1216, 64)] = jnp.zeros((64, SIDE), F32)
    put(0, dot3(feat[...].T, gp))
    put(128, dot3(agg[...].T, gp))
    put(256, dot3(ct[...], h))
    put(432, dot3(gt, h))
    packed[pl.ds(256 + CLS, 1)] = bias_one_grad[:, :SIDE]
    packed[pl.ds(608 + 256 + CLS, 1)] = bias_one_grad[:, SIDE:]
    packed[pl.ds(432 + CLS, 1)] = bias_two_grad[:, :SIDE]
    packed[pl.ds(608 + 432 + CLS, 1), : CLS - SIDE] = bias_two_grad[:, SIDE:]
    for dx in range(NX):
        for dy in range(NY):
            x = ((me >> 4) + dx) & 3
            y = ((me >> 2) + dy) & 3
            start = ((x * 4 + y) * 2 + (me & 1)) * 40
            same[dx, pl.ds(dy * 40, 40)] = packed[pl.ds(pl.multiple_of(start, 8), 40)]
            start = ((x * 4 + y) * 2 + (1 - (me & 1))) * 40
            other[dx, pl.ds(dy * 40, 40)] = packed[pl.ds(pl.multiple_of(start, 8), 40)]


def finish_kernel(place, q, qo, gs1, gn1, gb1, gs2, gn2, gb2, packed):
    me = place[0]
    for dx in range(NX):
        for dy in range(NY):
            x = ((me >> 4) + dx) & 3
            y = ((me >> 2) + dy) & 3
            start = ((x * 4 + y) * 2 + (me & 1)) * 40
            packed[pl.ds(pl.multiple_of(start, 8), 40)] = q[dx, pl.ds(dy * 40, 40)]
            start = ((x * 4 + y) * 2 + (1 - (me & 1))) * 40
            packed[pl.ds(pl.multiple_of(start, 8), 40)] = qo[dx, pl.ds(dy * 40, 40)]

    def take(start, rows):
        return jnp.concatenate(
            [packed[pl.ds(start, rows)], packed[pl.ds(608 + start, rows)]], axis=1
        )

    gs1[...] = take(0, 128)
    gn1[...] = take(128, 128)
    gs2[...] = take(256, CP).T[:, :CLS]
    gn2[...] = take(432, CP).T[:, :CLS]
    gb1[...] = take(256 + CLS, 1)
    gb2[...] = take(432 + CLS, 1)[:, :CLS]


def logits_kernel(z0, z1, z2, z3, base, out):
    total = (z0[...] + z1[...]) + (z2[...] + z3[...])
    out[...] = base[...] + total.T[:, :CLS]


def call(kernel, outs, ins, scratch=(), smem=0, any_from=None):
    specs = [SMEM] * smem + [VMEM] * (len(ins) - smem)
    if any_from is not None:
        specs[any_from:] = [ANY] * (len(ins) - any_from)
    return pl.pallas_call(
        kernel,
        out_shape=[jax.ShapeDtypeStruct(s, F32) for s in outs],
        in_specs=specs,
        out_specs=[VMEM] * len(outs),
        scratch_shapes=list(scratch),
        compiler_params=PARAMS,
    )(*ins)


def gather(block, half):
    other = send(block, dz=1)
    pieces = []
    for h in range(2):
        rows = slice(h * half, (h + 1) * half)
        pair = jnp.stack([block[rows], other[rows]])
        lane = [pair] + [send(pair, **shift(h == 0, -d)) for d in (1, 2, 3)]
        lane = jnp.stack(lane)
        plane = [lane] + [send(lane, **shift(h == 1, -d)) for d in (1, 2, 3)]
        swapped = [send(p, dc=1) for p in plane]
        pieces += [p.reshape(8, half, SIDE) for p in plane + swapped]
    return pieces


def scatter_plane(own, oth):
    halves = []
    for h in range(2):
        got = send(oth[h], dc=1)
        parts = [own[h][8 * d : 8 * d + 8] + got[8 * d : 8 * d + 8] for d in range(4)]
        parts = [parts[0]] + [send(parts[d], **shift(h == 0, d)) for d in (1, 2, 3)]
        q = (parts[0] + parts[1]) + (parts[2] + parts[3])
        parts = [q[2 * d : 2 * d + 2] for d in range(4)]
        parts = [parts[0]] + [send(parts[d], **shift(h == 1, d)) for d in (1, 2, 3)]
        halves.append((parts[0] + parts[1]) + (parts[2] + parts[3]))
    away = send(jnp.concatenate([halves[0][1], halves[1][1]], axis=0), dz=1)
    return halves[0][0], halves[1][0], away


def all_reduce(same, other):
    got = send(other, dc=1)
    parts = [same[d] + got[d] for d in range(4)]
    parts = [parts[0]] + [send(parts[d], dx=d) for d in (1, 2, 3)]
    q = (parts[0] + parts[1]) + (parts[2] + parts[3])
    parts = [q[40 * d : 40 * d + 40] for d in range(4)]
    parts = [parts[0]] + [send(parts[d], dy=d) for d in (1, 2, 3)]
    q = (parts[0] + parts[1]) + (parts[2] + parts[3])
    parts = [q] + [send_rep(q, d) for d in (1, 2, 3)]
    q = (parts[0] + parts[2]) + (parts[1] + parts[3])
    q = q + send(q, dz=1)
    lane = jnp.concatenate([q] + [send(q, dy=-d) for d in (1, 2, 3)], axis=0)
    plane = jnp.stack([lane] + [send(lane, dx=-d) for d in (1, 2, 3)])
    return plane, send(plane, dc=1)


def shards(
    features,
    tiles,
    columns,
    counts,
    self_one,
    neigh_one,
    bias_one,
    self_two,
    neigh_two,
    bias_two,
    cotangent,
):
    place = jnp.stack([lax.axis_index("row"), lax.axis_index("rep")]).astype(jnp.int32)
    columns = columns.reshape(4, 8)
    counts = counts.reshape(4)
    head = (place, columns, counts, tiles)
    block = (SIDE, SIDE)
    half_buf = lambda rows: pltpu.VMEM((64, rows, SIDE), F32)
    sems = pltpu.SemaphoreType.DMA((16,))

    (ct,) = call(transpose_kernel, [(CP, SIDE)], (cotangent,))
    pieces = gather(features, SIDE // 2)
    cts = [ct] + [send_rep(ct, -d) for d in (1, 2, 3)]

    out = (32, HP, SIDE)
    own0, own1, oth0, oth1 = call(transposed_kernel, [out] * 4, head + tuple(cts), smem=3)
    g0, g1, gz = scatter_plane((own0, own1), (oth0, oth1))

    parts = call(
        agg_one_kernel, [block] * 4, head + tuple(pieces),
        scratch=(half_buf(SIDE // 2), half_buf(SIDE // 2), sems), smem=3, any_from=4,
    )
    parts = [parts[0]] + [send_rep(parts[d], d) for d in (1, 2, 3)]
    agg, pre, yt = call(
        hidden_kernel, [block, (SIDE, 256), (CP, SIDE)],
        (*parts, features, self_one, neigh_one, bias_one.reshape(1, -1), neigh_two),
    )

    pieces = gather(yt, HP)
    base, same, other = call(
        grad_kernel, [(SIDE, CLS), (4, 160, SIDE), (4, 160, SIDE)],
        (place, g0, g1, gz, pre, agg, features, cotangent, ct, self_two, neigh_two,
         bias_two.reshape(1, -1)),
        scratch=(pltpu.VMEM((GROWS, SIDE), F32),), smem=1,
    )
    q, qo = all_reduce(same, other)
    gs1, gn1, gb1, gs2, gn2, gb2 = call(
        finish_kernel,
        [(128, 256), (128, 256), (1, 256), (256, CLS), (256, CLS), (1, CLS)],
        (place, q, qo), scratch=(pltpu.VMEM((GROWS, SIDE), F32),), smem=1,
    )

    parts = call(
        agg_two_kernel, [(CP, SIDE)] * 4, head + tuple(pieces),
        scratch=(half_buf(HP), half_buf(HP), sems), smem=3, any_from=4,
    )
    parts = [parts[0]] + [send_rep(parts[d], d) for d in (1, 2, 3)]
    (logits,) = call(logits_kernel, [(SIDE, CLS)], (*parts, base))
    return logits, gs1, gn1, gb1.reshape(-1), gs2, gn2, gb2.reshape(-1)


def solution(mesh):
    return jax.shard_map(
        shards,
        mesh=mesh,
        in_specs=(
            P(("row", "rep"), None),
            P("row", "rep", None, None, None),
            P("row", "rep", None),
            P("row", "rep"),
            P(),
            P(),
            P(),
            P(),
            P(),
            P(),
            P(("row", "rep"), None),
        ),
        out_specs=(P(("row", "rep"), None), P(), P(), P(), P(), P(), P()),
        check_vma=False,
    )
```

```python
import functools

import jax
import jax.numpy as jnp
from jax import lax
from jax.experimental import pallas as pl
from jax.experimental.pallas import tpu as pltpu
from jax.sharding import PartitionSpec as P

NX, NY, NZ, NC, NR = 4, 4, 2, 2, 4
SIDE = 128
CLS = 172
CP = 176
GROWS = 1280
F32 = jnp.float32
VMEM = pl.BlockSpec(memory_space=pltpu.VMEM)
SMEM = pl.BlockSpec(memory_space=pltpu.SMEM)
ANY = pl.BlockSpec(memory_space=pl.ANY)
MIB = 1024 * 1024


def row_perm(shift):
    pairs = []
    for x in range(NX):
        for y in range(NY):
            for z in range(NZ):
                for c in range(NC):
                    dx, dy, dz, dc = shift(c)
                    src = ((x * NY + y) * NZ + z) * NC + c
                    dst = (((x + dx) % NX * NY + (y + dy) % NY) * NZ + (z ^ dz)) * NC + (c ^ dc)
                    pairs.append((src, dst))
    return pairs


def send_core(a):
    return lax.ppermute(a, "row", row_perm(lambda c: (0, 0, 0, 1)))


def send_z(a):
    return lax.ppermute(a, "row", row_perm(lambda c: (0, 0, 1, 0)))


def send_plane(a, stage, d):
    return lax.ppermute(
        a, "row", row_perm(lambda c: (d, 0, 0, 0) if c == stage else (0, d, 0, 0))
    )


def send_rep(a, d):
    return lax.ppermute(a, "rep", [(j, (j + d) % NR) for j in range(NR)])


def split(a):
    hi = a.astype(jnp.bfloat16)
    lo = (a - hi.astype(F32)).astype(jnp.bfloat16)
    return hi, lo


def dot3(a, b, dims=((1,), (0,))):
    dn = (dims, ((), ()))
    ah, al = split(a)
    bh, bl = split(b)
    mm = lambda p, q: lax.dot_general(p, q, dn, preferred_element_type=F32)
    return mm(ah, bh) + (mm(ah, bl) + mm(al, bh))


def wide(a):
    return jnp.concatenate(split(a), axis=1)


def twice(a):
    w = wide(a)
    return jnp.concatenate([w, w], axis=0)


def twice_t(a):
    h, l = split(a)
    return jnp.concatenate(
        [jnp.concatenate([h, h], axis=1), jnp.concatenate([l, l], axis=1)], axis=0
    )


def fold(a):
    return a[:, :SIDE] + a[:, SIDE:]


def relative(c, me):
    diff = c ^ me
    dx = ((c >> 4) - (me >> 4)) & 3
    dy = ((c >> 2) - (me >> 2)) & 3
    core = c & 1
    d1 = jnp.where(core == 0, dx, dy)
    d2 = jnp.where(core == 0, dy, dx)
    return d1, d2, (diff >> 1) & 1, diff & 1


def live_tile(tile_buf, counts, block, s):
    t = tile_buf[block, 0, s]
    return jnp.where(s < counts[block], t, jnp.zeros_like(t))


def start_loads(refs, buf, tiles, tile_buf, sems):
    copies = [pltpu.make_async_copy(tiles, tile_buf, sems.at[len(refs)])]
    for k, ref in enumerate(refs):
        copies.append(pltpu.make_async_copy(ref, buf.at[pl.ds(k * 8, 8)], sems.at[k]))
    for c in copies:
        c.start()
    for c in copies:
        c.wait()


def agg_kernel(second, place, columns, counts, tiles, *rest):
    refs, outs, (buf, tile_buf, sems) = rest[:8], rest[8:12], rest[12:]
    me, rep = place[0], place[1]
    start_loads(refs, buf, tiles, tile_buf, sems)
    rows = buf.shape[1]
    for d in range(NR):
        block = (rep + d) & 3

        def step(i, acc, block=block):
            for u in range(2):
                s = 2 * i + u
                d1, d2, dz, dc = relative(columns[block, s], me)
                piece = buf[((dc * 4 + d2) * 4 + d1) * 2 + dz]
                tile = live_tile(tile_buf, counts, block, s)
                if second:
                    dn = (((1,), (1,)), ((), ()))
                    acc += lax.dot_general(
                        wide(piece), twice_t(tile), dn, preferred_element_type=F32
                    )
                else:
                    acc += jnp.dot(wide(tile), twice(piece), preferred_element_type=F32)
            return acc

        pairs = (counts[block] + 1) >> 1
        outs[d][...] = fold(lax.fori_loop(0, pairs, step, jnp.zeros((rows, 256), F32)))


def transposed_kernel(place, columns, counts, tiles, ct0, ct1, ct2, ct3,
                      own, oth0, oth1, oth2, oth3, tile_buf, ct_buf, sem):
    me, rep = place[0], place[1]
    copy = pltpu.make_async_copy(tiles, tile_buf, sem)
    copy.start()
    oths = (oth0, oth1, oth2, oth3)
    for o in (own,) + oths:
        o[...] = jnp.zeros(o.shape, F32)
    copy.wait()
    for d, ct in enumerate((ct0, ct1, ct2, ct3)):
        block = (rep + d) & 3
        ct_buf[...] = wide(ct[...])

        def step(i, _, block=block):
            done = []
            for u in range(2):
                s = 2 * i + u
                tile = live_tile(tile_buf, counts, block, s)
                done.append(
                    (s, fold(jnp.dot(ct_buf[...], twice(tile), preferred_element_type=F32)))
                )
            for s, r in done:
                d1, d2, dz, dc = relative(columns[block, s], me)
                at = d2 * 2 + dz

                @pl.when(dc == 0)
                def _():
                    own[d1 * 8 + at] += r

                for k in range(4):

                    @pl.when((dc != 0) & (d1 == k))
                    def _():
                        oths[k][at] += r

            return 0

        lax.fori_loop(0, (counts[block] + 1) >> 1, step, 0)


def hidden_kernel(a0, a1, a2, a3, feat, self_one, neigh_one, bias, nt, agg, pre, yt):
    total = (a0[...] + a1[...]) + (a2[...] + a3[...])
    agg[...] = total
    p = dot3(feat[...], self_one[...]) + dot3(total, neigh_one[...]) + bias[...]
    pre[...] = p
    h = p * jax.nn.sigmoid(p)
    yt[...] = dot3(nt[...], h, ((1,), (1,)))


def grad_kernel(place, g, gz, pre, agg, feat, ct, st, nt, bias_two, base, same, other, packed):
    me = place[0]
    p = pre[...]
    s = jax.nn.sigmoid(p)
    h = p * s
    base[...] = dot3(st[...], h, ((1,), (1,))) + jnp.broadcast_to(bias_two[...], (SIDE, CLS)).T
    gt = g[...] + gz[...]
    cot = ct[...].T
    gh = dot3(cot, st[...]) + dot3(gt.T, nt[...])
    gp = gh * s * (1.0 + p * (1.0 - s))
    bias_one_grad = jnp.sum(gp, axis=0, keepdims=True)
    bias_two_grad = jnp.sum(cot, axis=0, keepdims=True)

    def put(start, value):
        rows = value.shape[0]
        packed[pl.ds(start, rows)] = value[:, :SIDE]
        packed[pl.ds(608 + start, rows)] = value[:, SIDE:]

    for start in (424, 600, 1032, 1208):
        packed[pl.ds(start, 8)] = jnp.zeros((8, SIDE), F32)
    packed[pl.ds(1216, 64)] = jnp.zeros((64, SIDE), F32)
    put(0, dot3(feat[...].T, gp))
    put(128, dot3(agg[...].T, gp))
    put(256, dot3(ct[...], h))
    put(432, dot3(gt, h))
    packed[pl.ds(256 + CLS, 1)] = bias_one_grad[:, :SIDE]
    packed[pl.ds(608 + 256 + CLS, 1)] = bias_one_grad[:, SIDE:]
    packed[pl.ds(432 + CLS, 1)] = bias_two_grad[:, :SIDE]
    packed[pl.ds(608 + 432 + CLS, 1), : CLS - SIDE] = bias_two_grad[:, SIDE:]
    for slot, core, d1, d2, start in plane_order(me):
        (same, other)[slot][d1, pl.ds(d2 * 40, 40)] = packed[pl.ds(start, 40)]


def plane_order(me):
    for slot in range(2):
        core = (me & 1) ^ slot
        for d1 in range(4):
            for d2 in range(4):
                dx = jnp.where(core == 0, d1, d2)
                dy = jnp.where(core == 0, d2, d1)
                x = ((me >> 4) + dx) & 3
                y = ((me >> 2) + dy) & 3
                start = ((x * 4 + y) * 2 + core) * 40
                yield slot, core, d1, d2, pl.multiple_of(start, 8)


def finish_kernel(place, q, qo, gs1, gn1, gb1, gs2, gn2, gb2, packed):
    for slot, core, d1, d2, start in plane_order(place[0]):
        packed[pl.ds(start, 40)] = (q, qo)[slot][d1, pl.ds(d2 * 40, 40)]

    def take(start, rows):
        return jnp.concatenate(
            [packed[pl.ds(start, rows)], packed[pl.ds(608 + start, rows)]], axis=1
        )

    gs1[...] = take(0, 128)
    gn1[...] = take(128, 128)
    gs2[...] = take(256, CLS)
    gn2[...] = take(432, CLS)
    gb1[...] = take(256 + CLS, 1)
    gb2[...] = take(432 + CLS, 1)[:, :CLS]


def logits_kernel(z0, z1, z2, z3, base, out):
    out[...] = base[...] + ((z0[...] + z1[...]) + (z2[...] + z3[...]))


def call(kernel, outs, ins, scratch=(), smem=0, in_any=(), mib=8):
    specs = [SMEM] * smem + [VMEM] * (len(ins) - smem)
    for k in in_any:
        specs[k] = ANY
    return pl.pallas_call(
        kernel,
        out_shape=[jax.ShapeDtypeStruct(s, F32) for s in outs],
        in_specs=specs,
        out_specs=[VMEM] * len(outs),
        scratch_shapes=list(scratch),
        compiler_params=pltpu.CompilerParams(vmem_limit_bytes=mib * MIB),
    )(*ins)


def gather(block):
    pair = jnp.stack([block, send_z(block)])
    lane = jnp.concatenate([pair] + [send_plane(pair, 0, -d) for d in (1, 2, 3)])
    plane = [lane] + [send_plane(lane, 1, -d) for d in (1, 2, 3)]
    return plane + [send_core(p) for p in plane]


def scatter_plane(own, oth):
    parts = {}
    for d in (2, 1, 3, 0):
        parts[d] = own[8 * d : 8 * d + 8] + send_core(oth[d])
        if d:
            parts[d] = send_plane(parts[d], 0, d)
    q = (parts[0] + parts[1]) + (parts[2] + parts[3])
    parts = [q[:2]] + [send_plane(q[2 * d : 2 * d + 2], 1, d) for d in (1, 2, 3)]
    q = (parts[0] + parts[1]) + (parts[2] + parts[3])
    return q[0], send_z(q[1])


def all_reduce(same, other):
    got = send_core(other)
    parts = [same[d] + got[d] for d in range(4)]
    parts = [parts[0]] + [send_plane(parts[d], 0, d) for d in (1, 2, 3)]
    q = (parts[0] + parts[1]) + (parts[2] + parts[3])
    parts = [q[40 * d : 40 * d + 40] for d in range(4)]
    parts = [parts[0]] + [send_plane(parts[d], 1, d) for d in (1, 2, 3)]
    q = (parts[0] + parts[1]) + (parts[2] + parts[3])
    parts = [q] + [send_rep(q, d) for d in (1, 2, 3)]
    q = (parts[0] + parts[2]) + (parts[1] + parts[3])
    q = q + send_z(q)
    lane = jnp.concatenate([q] + [send_plane(q, 1, -d) for d in (1, 2, 3)], axis=0)
    plane = jnp.stack([lane] + [send_plane(lane, 0, -d) for d in (1, 2, 3)])
    return plane, send_core(plane)


def agg(second, head, pieces):
    rows = pieces[0].shape[1]
    shape = (rows, SIDE)
    parts = call(
        functools.partial(agg_kernel, second), [shape] * 4, head + tuple(pieces),
        scratch=(
            pltpu.VMEM((64, rows, SIDE), F32),
            pltpu.VMEM((4, 1, 8, SIDE, SIDE), F32),
            pltpu.SemaphoreType.DMA((9,)),
        ),
        smem=3, in_any=range(3, 12), mib=16,
    )
    return [parts[0]] + [send_rep(parts[d], d) for d in (1, 2, 3)]


def shards(
    features,
    tiles,
    columns,
    counts,
    self_one,
    neigh_one,
    bias_one,
    self_two,
    neigh_two,
    bias_two,
    cotangent,
):
    place = jnp.stack([lax.axis_index("row"), lax.axis_index("rep")]).astype(jnp.int32)
    head = (place, columns.reshape(4, 8), counts.reshape(4), tiles)
    block = (SIDE, SIDE)
    tall = (CLS, SIDE)
    ct, st, nt = cotangent.T, self_two.T, neigh_two.T

    pieces = gather(features)
    cts = [ct] + [send_rep(ct, -d) for d in (1, 2, 3)]
    own, *oth = call(
        transposed_kernel, [(32,) + tall] + [(8,) + tall] * 4, head + tuple(cts),
        scratch=(
            pltpu.VMEM((4, 1, 8, SIDE, SIDE), F32),
            pltpu.VMEM((CLS, 256), jnp.bfloat16),
            pltpu.SemaphoreType.DMA(()),
        ),
        smem=3, in_any=(3,), mib=16,
    )
    g, gz = scatter_plane(own, oth)

    sums, pre, yt = call(
        hidden_kernel, [block, (SIDE, 256), tall],
        (*agg(False, head, pieces), features, self_one, neigh_one, bias_one.reshape(1, -1), nt),
    )
    pieces = gather(yt)
    base, same, other = call(
        grad_kernel, [tall, (4, 160, SIDE), (4, 160, SIDE)],
        (place, g, gz, pre, sums, features, ct, st, nt, bias_two.reshape(1, -1)),
        scratch=(pltpu.VMEM((GROWS, SIDE), F32),), smem=1,
    )
    q, qo = all_reduce(same, other)
    gs1, gn1, gb1, gs2, gn2, gb2 = call(
        finish_kernel,
        [(128, 256), (128, 256), (1, 256), (CLS, 256), (CLS, 256), (1, CLS)],
        (place, q, qo), scratch=(pltpu.VMEM((GROWS, SIDE), F32),), smem=1,
    )
    (logits,) = call(logits_kernel, [tall], (*agg(True, head, pieces), base))
    return logits.T, gs1, gn1, gb1.reshape(-1), gs2.T, gn2.T, gb2.reshape(-1)


def solution(mesh):
    return jax.shard_map(
        shards,
        mesh=mesh,
        in_specs=(
            P(("row", "rep"), None),
            P("row", "rep", None, None, None),
            P("row", "rep", None),
            P("row", "rep"),
            P(),
            P(),
            P(),
            P(),
            P(),
            P(),
            P(("row", "rep"), None),
        ),
        out_specs=(P(("row", "rep"), None), P(), P(), P(), P(), P(), P()),
        check_vma=False,
    )
```

```python
import functools

import jax
import jax.numpy as jnp
from jax import lax
from jax.experimental import pallas as pl
from jax.experimental.pallas import tpu as pltpu
from jax.sharding import PartitionSpec as P

NX, NY, NZ, NC, NR = 4, 4, 2, 2, 4
SIDE = 128
CLS = 172
CP = 176
GROWS = 1280
F32 = jnp.float32
VMEM = pl.BlockSpec(memory_space=pltpu.VMEM)
SMEM = pl.BlockSpec(memory_space=pltpu.SMEM)
ANY = pl.BlockSpec(memory_space=pl.ANY)
MIB = 1024 * 1024
COUNTS, ME, REP = 32, 36, 37


def row_perm(shift):
    pairs = []
    for x in range(NX):
        for y in range(NY):
            for z in range(NZ):
                for c in range(NC):
                    dx, dy, dz, dc = shift(c)
                    src = ((x * NY + y) * NZ + z) * NC + c
                    dst = (((x + dx) % NX * NY + (y + dy) % NY) * NZ + (z ^ dz)) * NC + (c ^ dc)
                    pairs.append((src, dst))
    return pairs


def send_core(a):
    return lax.ppermute(a, "row", row_perm(lambda c: (0, 0, 0, 1)))


def send_z(a):
    return lax.ppermute(a, "row", row_perm(lambda c: (0, 0, 1, 0)))


def send_plane(a, stage, d):
    return lax.ppermute(
        a, "row", row_perm(lambda c: (d, 0, 0, 0) if c == stage else (0, d, 0, 0))
    )


def send_rep(a, d):
    return lax.ppermute(a, "rep", [(j, (j + d) % NR) for j in range(NR)])


def swap_rep(a, bit):
    return lax.ppermute(a, "rep", [(j, j ^ bit) for j in range(NR)])


def split(a):
    hi = a.astype(jnp.bfloat16)
    lo = (a - hi.astype(F32)).astype(jnp.bfloat16)
    return hi, lo


def dot3(a, b, dims=((1,), (0,))):
    dn = (dims, ((), ()))
    ah, al = split(a)
    bh, bl = split(b)
    mm = lambda p, q: lax.dot_general(p, q, dn, preferred_element_type=F32)
    return mm(ah, bh) + (mm(ah, bl) + mm(al, bh))


def wide(a):
    return jnp.concatenate(split(a), axis=1)


def twice(a):
    w = wide(a)
    return jnp.concatenate([w, w], axis=0)


def twice_t(a):
    h, l = split(a)
    return jnp.concatenate(
        [jnp.concatenate([h, h], axis=1), jnp.concatenate([l, l], axis=1)], axis=0
    )


def fold(a):
    return a[:, :SIDE] + a[:, SIDE:]


def relative(c, me):
    diff = c ^ me
    dx = ((c >> 4) - (me >> 4)) & 3
    dy = ((c >> 2) - (me >> 2)) & 3
    core = c & 1
    d1 = jnp.where(core == 0, dx, dy)
    d2 = jnp.where(core == 0, dy, dx)
    return d1, d2, (diff >> 1) & 1, diff & 1


def live_tile(tile_buf, meta, block, s):
    t = tile_buf[block, 0, s]
    return jnp.where(s < meta[COUNTS + block], t, jnp.zeros_like(t))


def start_loads(refs, buf, tiles, tile_buf, sems):
    copies = [pltpu.make_async_copy(tiles, tile_buf, sems.at[len(refs)])]
    start = 0
    for k, ref in enumerate(refs):
        size = ref.shape[0]
        copies.append(pltpu.make_async_copy(ref, buf.at[pl.ds(start, size)], sems.at[k]))
        start += size
    for c in copies:
        c.start()
    for c in copies:
        c.wait()


def agg_kernel(second, meta, tiles, *rest):
    refs, outs, (buf, tile_buf, sems) = rest[:6], rest[6:10], rest[10:]
    me, rep = meta[ME], meta[REP]
    start_loads(refs, buf, tiles, tile_buf, sems)
    rows = buf.shape[1]
    for d in range(NR):
        block = (rep + d) & 3

        def step(i, acc, block=block):
            for u in range(2):
                s = 2 * i + u
                d1, d2, dz, dc = relative(meta[block * 8 + s], me)
                piece = buf[((dc * 4 + d2) * 4 + d1) * 2 + dz]
                tile = live_tile(tile_buf, meta, block, s)
                if second:
                    dn = (((1,), (1,)), ((), ()))
                    acc += lax.dot_general(
                        wide(piece), twice_t(tile), dn, preferred_element_type=F32
                    )
                else:
                    acc += jnp.dot(wide(tile), twice(piece), preferred_element_type=F32)
            return acc

        pairs = (meta[COUNTS + block] + 1) >> 1
        outs[d][...] = fold(lax.fori_loop(0, pairs, step, jnp.zeros((rows, 256), F32)))


def transposed_kernel(meta, tiles, ct0, ct1, ct2, ct3, own, oth, tile_buf, ct_buf, sem):
    me, rep = meta[ME], meta[REP]
    copy = pltpu.make_async_copy(tiles, tile_buf, sem)
    copy.start()
    for o in (own, oth):
        o[...] = jnp.zeros(o.shape, F32)
    copy.wait()
    for d, ct in enumerate((ct0, ct1, ct2, ct3)):
        block = (rep + d) & 3
        ct_buf[...] = jnp.concatenate(
            [wide(ct[...]), jnp.zeros((CP - CLS, 256), jnp.bfloat16)], axis=0
        )

        def step(i, _, block=block):
            done = []
            for u in range(2):
                s = 2 * i + u
                tile = live_tile(tile_buf, meta, block, s)
                done.append(
                    (s, fold(jnp.dot(ct_buf[...], twice(tile), preferred_element_type=F32)))
                )
            for s, r in done:
                d1, d2, dz, dc = relative(meta[block * 8 + s], me)
                at = (d1 * 4 + d2) * 2 + dz

                @pl.when(dc == 0)
                def _():
                    own[at] += r

                @pl.when(dc != 0)
                def _():
                    oth[at] += r

            return 0

        lax.fori_loop(0, (meta[COUNTS + block] + 1) >> 1, step, 0)


def hidden_kernel(a0, a1, a2, a3, feat, self_one, neigh_one, bias, nt, agg, pre, yt):
    total = (a0[...] + a1[...]) + (a2[...] + a3[...])
    agg[...] = total
    p = dot3(feat[...], self_one[...]) + dot3(total, neigh_one[...]) + bias[...]
    pre[...] = p
    h = p * jax.nn.sigmoid(p)
    yt[pl.ds(CP - 8, 8)] = jnp.zeros((8, SIDE), F32)
    yt[pl.ds(0, CLS)] = dot3(nt[...], h, ((1,), (1,)))


def grad_kernel(meta, g, gz, pre, agg, feat, ct, st, nt, bias_two, base, same, other, packed):
    p = pre[...]
    s = jax.nn.sigmoid(p)
    h = p * s
    base[...] = dot3(st[...], h, ((1,), (1,))) + jnp.broadcast_to(bias_two[...], (SIDE, CLS)).T
    gt = g[pl.ds(0, CLS)] + gz[pl.ds(0, CLS)]
    cot = ct[...].T
    gh = dot3(cot, st[...]) + dot3(gt.T, nt[...])
    gp = gh * s * (1.0 + p * (1.0 - s))
    bias_one_grad = jnp.sum(gp, axis=0, keepdims=True)
    bias_two_grad = jnp.sum(cot, axis=0, keepdims=True)

    def put(start, value):
        rows = value.shape[0]
        packed[pl.ds(start, rows)] = value[:, :SIDE]
        packed[pl.ds(608 + start, rows)] = value[:, SIDE:]

    for start in (424, 600, 1032, 1208):
        packed[pl.ds(start, 8)] = jnp.zeros((8, SIDE), F32)
    packed[pl.ds(1216, 64)] = jnp.zeros((64, SIDE), F32)
    put(0, dot3(feat[...].T, gp))
    put(128, dot3(agg[...].T, gp))
    put(256, dot3(ct[...], h))
    put(432, dot3(gt, h))
    packed[pl.ds(256 + CLS, 1)] = bias_one_grad[:, :SIDE]
    packed[pl.ds(608 + 256 + CLS, 1)] = bias_one_grad[:, SIDE:]
    packed[pl.ds(432 + CLS, 1)] = bias_two_grad[:, :SIDE]
    packed[pl.ds(608 + 432 + CLS, 1), : CLS - SIDE] = bias_two_grad[:, SIDE:]
    for slot, d, start in piece_order(meta):
        (same, other)[slot][d] = packed[pl.ds(start, 160)]


def piece_order(meta):
    for slot in range(2):
        for d in range(NR):
            start = (((meta[ME] & 1) ^ slot) * NR + (meta[REP] ^ d)) * 160
            yield slot, d, pl.multiple_of(start, 8)


def finish_kernel(meta, q, qo, gs1, gn1, gb1, gs2, gn2, gb2, packed):
    for slot, d, start in piece_order(meta):
        packed[pl.ds(start, 160)] = (q, qo)[slot][(0, 2, 1, 3)[d]]

    def take(start, rows):
        return jnp.concatenate(
            [packed[pl.ds(start, rows)], packed[pl.ds(608 + start, rows)]], axis=1
        )

    gs1[...] = take(0, 128)
    gn1[...] = take(128, 128)
    gs2[...] = take(256, CLS)
    gn2[...] = take(432, CLS)
    gb1[...] = take(256 + CLS, 1)
    gb2[...] = take(432 + CLS, 1)[:, :CLS]


def logits_kernel(z0, z1, z2, z3, base, out):
    total = (z0[...] + z1[...]) + (z2[...] + z3[...])
    out[...] = base[...] + total[:CLS]


def call(kernel, outs, ins, scratch=(), smem=0, in_any=(), mib=8, cost=6):
    specs = [SMEM] * smem + [VMEM] * (len(ins) - smem)
    for k in in_any:
        specs[k] = ANY
    return pl.pallas_call(
        kernel,
        out_shape=[jax.ShapeDtypeStruct(s, F32) for s in outs],
        in_specs=specs,
        out_specs=[VMEM] * len(outs),
        scratch_shapes=list(scratch),
        cost_estimate=pl.CostEstimate(flops=0, bytes_accessed=cost * MIB, transcendentals=0),
        compiler_params=pltpu.CompilerParams(vmem_limit_bytes=mib * MIB),
    )(*ins)


def after(a, *others):
    return lax.optimization_barrier((a, *others))[0]


def add4(a, b, c, d):
    return (a + b) + (c + d)


def gather_lane(block, swapped, *held):
    pair = after(jnp.stack([block, swapped]), *held)
    return jnp.concatenate([pair] + [send_plane(pair, 0, -d) for d in (1, 2, 3)])


def gather_plane(lane):
    return [lane] + [send_plane(lane, 1, -d) for d in (1, 2, 3)]


def gather_core(plane, *held):
    rest = jnp.concatenate([after(plane[1], *held)] + plane[2:])
    return plane + [send_core(plane[0]), send_core(rest)]


def scatter_core(own, oth):
    got = send_core(oth)
    return [own[8 * d : 8 * d + 8] + got[8 * d : 8 * d + 8] for d in range(4)]


def scatter_lane(parts, *held):
    return [parts[0]] + [send_plane(after(parts[d], *held), 0, d) for d in (1, 2, 3)]


def scatter_plane(q):
    q = add4(q[:2], *(send_plane(q[2 * d : 2 * d + 2], 1, d) for d in (1, 2, 3)))
    return q[0], send_z(q[1])


def reduce_reps(same, other):
    got = send_core(other)
    kept = jnp.stack([same[0] + got[0], same[2] + got[2]])
    kept = kept + swap_rep(jnp.stack([same[1] + got[1], same[3] + got[3]]), 1)
    q = kept[0] + swap_rep(kept[1], 2)
    return q + send_z(q)


def all_reduce(q, products, held):
    q = add4(after(q, products[0]), *(send_plane(q, 1, d) for d in (1, 2, 3)))
    q = after(q, held[1])
    q = after(jnp.stack([q, swap_rep(q, 2)]), *held[2:])
    q = jnp.concatenate([q, swap_rep(q, 1)])
    return q, send_core(q)


def agg(second, head, pieces):
    rows = pieces[0].shape[1]
    shape = (rows, SIDE)
    return call(
        functools.partial(agg_kernel, second), [shape] * 4, head + tuple(pieces),
        scratch=(
            pltpu.VMEM((64, rows, SIDE), F32),
            pltpu.VMEM((4, 1, 8, SIDE, SIDE), F32),
            pltpu.SemaphoreType.DMA((7,)),
        ),
        smem=1, in_any=range(1, 8), mib=16, cost=12,
    )


def sum_reps(parts, *held):
    return [parts[0]] + [send_rep(after(parts[d], *held), d) for d in (1, 2, 3)]


def shards(
    features,
    tiles,
    columns,
    counts,
    self_one,
    neigh_one,
    bias_one,
    self_two,
    neigh_two,
    bias_two,
    cotangent,
):
    place = jnp.stack([lax.axis_index("row"), lax.axis_index("rep")]).astype(jnp.int32)
    meta = jnp.concatenate([columns.reshape(-1), counts.reshape(-1), place])
    head = (meta, tiles)
    block = (SIDE, SIDE)
    tall, padded = (CLS, SIDE), (CP, SIDE)
    ct, st, nt = cotangent.T, self_two.T, neigh_two.T

    swapped = send_z(features)
    cts = [ct] + [after(send_rep(ct, -d), swapped) for d in (1, 2, 3)]
    lane = gather_lane(features, swapped)
    own, oth = call(
        transposed_kernel, [(32,) + padded] * 2, head + tuple(after(c, lane) for c in cts),
        scratch=(
            pltpu.VMEM((4, 1, 8, SIDE, SIDE), F32),
            pltpu.VMEM((CP, 256), jnp.bfloat16),
            pltpu.SemaphoreType.DMA(()),
        ),
        smem=1, in_any=(1,), mib=16, cost=12,
    )
    plane = gather_plane(lane)
    parts = scatter_core(own, oth)
    laned = scatter_lane(parts, *plane[1:])
    products = agg(False, head, gather_core(plane, *parts))
    q = add4(after(laned[0], products[0]), *laned[1:])

    sums, pre, yt = call(
        hidden_kernel, [block, (SIDE, 256), padded],
        (*sum_reps(products, q), features, self_one, neigh_one, bias_one.reshape(1, -1), nt),
    )
    g, gz = scatter_plane(q)
    plane = gather_plane(gather_lane(yt, send_z(yt), gz))
    base, same, other = call(
        grad_kernel, [tall, (4, 160, SIDE), (4, 160, SIDE)],
        (meta, g, gz, pre, sums, features, ct, st, nt, bias_two.reshape(1, -1)),
        scratch=(pltpu.VMEM((GROWS, SIDE), F32),), smem=1,
    )
    kept = reduce_reps(same, other)
    pieces = gather_core(plane, kept)
    kept = add4(kept, *(send_plane(kept, 0, d) for d in (1, 2, 3)))
    pieces[-1] = after(pieces[-1], kept)
    products = agg(True, head, pieces)
    parts = sum_reps(products)
    (logits,) = call(logits_kernel, [tall], (*parts, base))
    q, qo = all_reduce(kept, products, parts)
    gs1, gn1, gb1, gs2, gn2, gb2 = call(
        finish_kernel,
        [(128, 256), (128, 256), (1, 256), (CLS, 256), (CLS, 256), (1, CLS)],
        (meta, q, qo), scratch=(pltpu.VMEM((GROWS, SIDE), F32),), smem=1,
    )
    return logits.T, gs1, gn1, gb1.reshape(-1), gs2.T, gn2.T, gb2.reshape(-1)


def solution(mesh):
    return jax.shard_map(
        shards,
        mesh=mesh,
        in_specs=(
            P(("row", "rep"), None),
            P("row", "rep", None, None, None),
            P("row", "rep", None),
            P("row", "rep"),
            P(),
            P(),
            P(),
            P(),
            P(),
            P(),
            P(("row", "rep"), None),
        ),
        out_specs=(P(("row", "rep"), None), P(), P(), P(), P(), P(), P()),
        check_vma=False,
    )
```

```python
import functools

import jax
import jax.numpy as jnp
from jax import lax
from jax.experimental import pallas as pl
from jax.experimental.pallas import tpu as pltpu
from jax.sharding import PartitionSpec as P

NX, NY, NZ, NC, NR = 4, 4, 2, 2, 4
SIDE = 128
CLS = 172
CP = 176
GROWS = 1280
F32 = jnp.float32
VMEM = pl.BlockSpec(memory_space=pltpu.VMEM)
SMEM = pl.BlockSpec(memory_space=pltpu.SMEM)
ANY = pl.BlockSpec(memory_space=pl.ANY)
HBM = pl.BlockSpec(memory_space=pltpu.HBM)
MIB = 1024 * 1024
COUNTS, ME, REP = 32, 36, 37


def row_perm(shift):
    pairs = []
    for x in range(NX):
        for y in range(NY):
            for z in range(NZ):
                for c in range(NC):
                    dx, dy, dz, dc = shift(c)
                    src = ((x * NY + y) * NZ + z) * NC + c
                    dst = (((x + dx) % NX * NY + (y + dy) % NY) * NZ + (z ^ dz)) * NC + (c ^ dc)
                    pairs.append((src, dst))
    return pairs


def send_core(a):
    return lax.ppermute(a, "row", row_perm(lambda c: (0, 0, 0, 1)))


def send_z(a):
    return lax.ppermute(a, "row", row_perm(lambda c: (0, 0, 1, 0)))


def send_plane(a, stage, d):
    return lax.ppermute(
        a, "row", row_perm(lambda c: (d, 0, 0, 0) if c == stage else (0, d, 0, 0))
    )


def send_rep(a, d):
    return lax.ppermute(a, "rep", [(j, (j + d) % NR) for j in range(NR)])


def swap_rep(a, bit):
    return lax.ppermute(a, "rep", [(j, j ^ bit) for j in range(NR)])


def split(a):
    hi = a.astype(jnp.bfloat16)
    lo = (a - hi.astype(F32)).astype(jnp.bfloat16)
    return hi, lo


def dot3(a, b, dims=((1,), (0,))):
    dn = (dims, ((), ()))
    ah, al = split(a)
    bh, bl = split(b)
    mm = lambda p, q: lax.dot_general(p, q, dn, preferred_element_type=F32)
    return mm(ah, bh) + (mm(ah, bl) + mm(al, bh))


def wide(a):
    return jnp.concatenate(split(a), axis=1)


def twice(a):
    w = wide(a)
    return jnp.concatenate([w, w], axis=0)


def twice_t(a):
    h, l = split(a)
    return jnp.concatenate(
        [jnp.concatenate([h, h], axis=1), jnp.concatenate([l, l], axis=1)], axis=0
    )


def fold(a):
    return a[:, :SIDE] + a[:, SIDE:]


def relative(c, me):
    diff = c ^ me
    dx = ((c >> 4) - (me >> 4)) & 3
    dy = ((c >> 2) - (me >> 2)) & 3
    core = c & 1
    d1 = jnp.where(core == 0, dx, dy)
    d2 = jnp.where(core == 0, dy, dx)
    return d1, d2, (diff >> 1) & 1, diff & 1


def live_tile(tile_buf, meta, block, s):
    t = tile_buf[block, 0, s]
    return jnp.where(s < meta[COUNTS + block], t, jnp.zeros_like(t))


def start_loads(refs, buf, tiles, tile_buf, sems):
    copies = [pltpu.make_async_copy(tiles, tile_buf, sems.at[len(refs)])]
    start = 0
    for k, ref in enumerate(refs):
        size = ref.shape[0]
        copies.append(pltpu.make_async_copy(ref, buf.at[pl.ds(start, size)], sems.at[k]))
        start += size
    for c in copies:
        c.start()
    for c in copies:
        c.wait()


def agg_kernel(second, meta, tiles, *rest):
    refs, outs, (buf, tile_buf, sems) = rest[:6], rest[6:8], rest[8:]
    me, rep = meta[ME], meta[REP]
    start_loads(refs, buf, tiles, tile_buf, sems)
    rows = buf.shape[1]
    for d in range(NR):
        block = rep ^ d

        def step(i, acc, block=block):
            for u in range(2):
                s = 2 * i + u
                d1, d2, dz, dc = relative(meta[block * 8 + s], me)
                piece = buf[((dc * 4 + d2) * 4 + d1) * 2 + dz]
                tile = live_tile(tile_buf, meta, block, s)
                if second:
                    dn = (((1,), (1,)), ((), ()))
                    acc += lax.dot_general(
                        wide(piece), twice_t(tile), dn, preferred_element_type=F32
                    )
                else:
                    acc += jnp.dot(wide(tile), twice(piece), preferred_element_type=F32)
            return acc

        pairs = (meta[COUNTS + block] + 1) >> 1
        outs[d & 1][d >> 1] = fold(lax.fori_loop(0, pairs, step, jnp.zeros((rows, 256), F32)))


def transposed_kernel(meta, tiles, near, far, own, oth, tile_buf, ct_buf, sem):
    me, rep = meta[ME], meta[REP]
    copy = pltpu.make_async_copy(tiles, tile_buf, sem)
    copy.start()
    for o in (own, oth):
        o[...] = jnp.zeros(o.shape, F32)
    copy.wait()
    for d in range(NR):
        block = rep ^ d
        ct_buf[...] = jnp.concatenate(
            [wide((near, far)[d & 1][d >> 1]), jnp.zeros((CP - CLS, 256), jnp.bfloat16)], axis=0
        )

        def step(i, _, block=block):
            done = []
            for u in range(2):
                s = 2 * i + u
                tile = live_tile(tile_buf, meta, block, s)
                done.append(
                    (s, fold(jnp.dot(ct_buf[...], twice(tile), preferred_element_type=F32)))
                )
            for s, r in done:
                d1, d2, dz, dc = relative(meta[block * 8 + s], me)
                at = (d1 * 4 + d2) * 2 + dz

                @pl.when(dc == 0)
                def _():
                    own[at] += r

                @pl.when(dc != 0)
                def _():
                    oth[at] += r

            return 0

        lax.fori_loop(0, (meta[COUNTS + block] + 1) >> 1, step, 0)


def hidden_kernel(kept, got, last, feat, self_one, neigh_one, bias, nt, agg, pre, yt):
    total = (kept[0] + got[0]) + last[...]
    agg[...] = total
    p = dot3(feat[...], self_one[...]) + dot3(total, neigh_one[...]) + bias[...]
    pre[...] = p
    h = p * jax.nn.sigmoid(p)
    yt[pl.ds(CP - 8, 8)] = jnp.zeros((8, SIDE), F32)
    yt[pl.ds(0, CLS)] = dot3(nt[...], h, ((1,), (1,)))


def grad_kernel(meta, g, gz, pre, agg, feat, ct, st, nt, bias_two, base, same, other, packed):
    p = pre[...]
    s = jax.nn.sigmoid(p)
    h = p * s
    base[...] = dot3(st[...], h, ((1,), (1,))) + jnp.broadcast_to(bias_two[...], (SIDE, CLS)).T
    gt = g[pl.ds(0, CLS)] + gz[pl.ds(0, CLS)]
    cot = ct[...].T
    gh = dot3(cot, st[...]) + dot3(gt.T, nt[...])
    gp = gh * s * (1.0 + p * (1.0 - s))
    bias_one_grad = jnp.sum(gp, axis=0, keepdims=True)
    bias_two_grad = jnp.sum(cot, axis=0, keepdims=True)

    def put(start, value):
        rows = value.shape[0]
        packed[pl.ds(start, rows)] = value[:, :SIDE]
        packed[pl.ds(608 + start, rows)] = value[:, SIDE:]

    for start in (424, 600, 1032, 1208):
        packed[pl.ds(start, 8)] = jnp.zeros((8, SIDE), F32)
    packed[pl.ds(1216, 64)] = jnp.zeros((64, SIDE), F32)
    put(0, dot3(feat[...].T, gp))
    put(128, dot3(agg[...].T, gp))
    put(256, dot3(ct[...], h))
    put(432, dot3(gt, h))
    packed[pl.ds(256 + CLS, 1)] = bias_one_grad[:, :SIDE]
    packed[pl.ds(608 + 256 + CLS, 1)] = bias_one_grad[:, SIDE:]
    packed[pl.ds(432 + CLS, 1)] = bias_two_grad[:, :SIDE]
    packed[pl.ds(608 + 432 + CLS, 1), : CLS - SIDE] = bias_two_grad[:, SIDE:]
    for slot, d, start in piece_order(meta):
        (same, other)[slot][d] = packed[pl.ds(start, 160)]


def piece_order(meta):
    me = meta[ME]
    for slot in range(2):
        core = (me & 1) ^ slot
        at = jnp.where(core == 0, me >> 4, me >> 2)
        for d in range(4):
            start = (core * 4 + ((at + d) & 3)) * 160
            yield slot, d, pl.multiple_of(start, 8)


def finish_kernel(meta, q, qo, gs1, gn1, gb1, gs2, gn2, gb2, packed):
    for slot, d, start in piece_order(meta):
        packed[pl.ds(start, 160)] = (q, qo)[slot][d]

    def take(start, rows):
        return jnp.concatenate(
            [packed[pl.ds(start, rows)], packed[pl.ds(608 + start, rows)]], axis=1
        )

    gs1[...] = take(0, 128)
    gn1[...] = take(128, 128)
    gs2[...] = take(256, CLS)
    gn2[...] = take(432, CLS)
    gb1[...] = take(256 + CLS, 1)
    gb2[...] = take(432 + CLS, 1)[:, :CLS]


def logits_kernel(kept, got, last, base, out):
    part = pl.ds(0, CLS)
    out[...] = base[...] + ((kept[0, part] + got[0, part]) + last[part])


def call(kernel, outs, ins, scratch=(), smem=0, in_hbm=(), in_any=(), mib=8, cost=6):
    specs = [SMEM] * smem + [VMEM] * (len(ins) - smem)
    for k in in_any:
        specs[k] = ANY
    for k in in_hbm:
        specs[k] = HBM
    return pl.pallas_call(
        kernel,
        out_shape=[jax.ShapeDtypeStruct(s, F32) for s in outs],
        in_specs=specs,
        out_specs=[VMEM] * len(outs),
        scratch_shapes=list(scratch),
        cost_estimate=pl.CostEstimate(flops=0, bytes_accessed=cost * MIB, transcendentals=0),
        compiler_params=pltpu.CompilerParams(vmem_limit_bytes=mib * MIB),
    )(*ins)


def after(a, *others):
    return lax.optimization_barrier((a, *others))[0]


def add4(a, b, c, d):
    return (a + b) + (c + d)


def gather_lane(block, swapped, *held):
    pair = after(jnp.stack([block, swapped]), *held)
    return jnp.concatenate([pair] + [send_plane(pair, 0, -d) for d in (1, 2, 3)])


def gather_plane(lane):
    return [lane] + [send_plane(lane, 1, -d) for d in (1, 2, 3)]


def gather_ring(lane):
    one, three = send_plane(lane, 1, 3), send_plane(lane, 1, 1)
    two = jnp.concatenate([send_plane(one[:4], 1, 3), send_plane(three[4:], 1, 1)])
    return [lane, one, two, three]


def gather_core(plane, *held):
    rest = jnp.concatenate([after(plane[1], *held)] + plane[2:])
    return plane + [send_core(plane[0]), send_core(rest)]


def scatter_core(own, oth):
    got = send_core(oth)
    return [own[8 * d : 8 * d + 8] + got[8 * d : 8 * d + 8] for d in range(4)]


def scatter_lane(parts, *held):
    one, three = send_plane(parts[1], 0, 1), send_plane(parts[3], 0, 3)
    return [parts[0], one, send_plane(after(parts[2], *held), 0, 2), three]


def scatter_plane(q):
    q = add4(q[:2], *(send_plane(q[2 * d : 2 * d + 2], 1, d) for d in (1, 2, 3)))
    return q[0], send_z(q[1])


def reduce_lane(same, other):
    got = send_core(other)
    parts = [same[d] + got[d] for d in range(4)]
    return add4(parts[0], *(send_plane(parts[d], 0, d) for d in (1, 2, 3)))


def last_sums(q, products):
    kept, given = products
    got = swap_rep(given, 1)
    last = swap_rep(kept[1] + got[1], 2)
    q = after(q, kept) + send_z(q)
    q = add4(q, *(send_plane(q, 1, d) for d in (1, 2, 3)))
    q = after(q, got)
    q = jnp.stack([q] + [send_plane(q, 0, -d) for d in (1, 2, 3)])
    q = after(q, last)
    return kept, got, last, q, send_core(q)


def agg(second, head, pieces):
    rows = pieces[0].shape[1]
    shape = (rows, SIDE)
    return call(
        functools.partial(agg_kernel, second), [(2,) + shape] * 2, head + tuple(pieces),
        scratch=(
            pltpu.VMEM((64, rows, SIDE), F32),
            pltpu.VMEM((4, 1, 8, SIDE, SIDE), F32),
            pltpu.SemaphoreType.DMA((7,)),
        ),
        smem=1, in_hbm=(1,), in_any=range(2, 8), mib=16, cost=12,
    )


def shards(
    features,
    tiles,
    columns,
    counts,
    self_one,
    neigh_one,
    bias_one,
    self_two,
    neigh_two,
    bias_two,
    cotangent,
):
    place = jnp.stack([lax.axis_index("row"), lax.axis_index("rep")]).astype(jnp.int32)
    meta = jnp.concatenate([columns.reshape(-1), counts.reshape(-1), place])
    head = (meta, tiles)
    block = (SIDE, SIDE)
    tall, padded = (CLS, SIDE), (CP, SIDE)
    ct, st, nt = cotangent.T, self_two.T, neigh_two.T

    swapped = send_z(features)
    pair = jnp.stack([ct, swap_rep(ct, 2)])
    far = swap_rep(pair, 1)
    lane = gather_lane(features, swapped)
    own, oth = call(
        transposed_kernel, [(32,) + padded] * 2, head + (after(pair, lane), far),
        scratch=(
            pltpu.VMEM((4, 1, 8, SIDE, SIDE), F32),
            pltpu.VMEM((CP, 256), jnp.bfloat16),
            pltpu.SemaphoreType.DMA(()),
        ),
        smem=1, in_hbm=(1,), mib=16, cost=12,
    )
    plane = gather_plane(lane)
    parts = scatter_core(own, oth)
    laned = scatter_lane(parts, *plane[1:])
    pieces = gather_core(plane, *parts)
    products = agg(False, head, pieces)

    kept, given = products
    got = swap_rep(given, 1)
    last = swap_rep(kept[1] + got[1], 2)
    q = add4(after(laned[0], got), *laned[1:])
    sums, pre, yt = call(
        hidden_kernel, [block, (SIDE, 256), padded],
        (kept, got, last, features, self_one, neigh_one, bias_one.reshape(1, -1), nt),
    )
    g, gz = scatter_plane(q)
    lane = gather_lane(yt, send_z(yt))
    base, same, other = call(
        grad_kernel, [tall, (4, 160, SIDE), (4, 160, SIDE)],
        (meta, g, gz, after(pre, lane), sums, features, ct, st, nt, bias_two.reshape(1, -1)),
        scratch=(pltpu.VMEM((GROWS, SIDE), F32),), smem=1,
    )
    plane = gather_plane(after(lane, same))
    kept = reduce_lane(same, other)
    kept = kept + swap_rep(kept, 1)
    pieces = gather_core(plane, kept)
    kept = kept + swap_rep(kept, 2)
    pieces[-1] = after(pieces[-1], kept)
    products = agg(True, head, pieces)
    *parts, q, qo = last_sums(kept, products)
    (logits,) = call(logits_kernel, [tall], (*parts, base))
    gs1, gn1, gb1, gs2, gn2, gb2 = call(
        finish_kernel,
        [(128, 256), (128, 256), (1, 256), (CLS, 256), (CLS, 256), (1, CLS)],
        (meta, q, qo), scratch=(pltpu.VMEM((GROWS, SIDE), F32),), smem=1,
    )
    return logits.T, gs1, gn1, gb1.reshape(-1), gs2.T, gn2.T, gb2.reshape(-1)


def solution(mesh):
    return jax.shard_map(
        shards,
        mesh=mesh,
        in_specs=(
            P(("row", "rep"), None),
            P("row", "rep", None, None, None),
            P("row", "rep", None),
            P("row", "rep"),
            P(),
            P(),
            P(),
            P(),
            P(),
            P(),
            P(("row", "rep"), None),
        ),
        out_specs=(P(("row", "rep"), None), P(), P(), P(), P(), P(), P()),
        check_vma=False,
    )
```

```python
import functools

import jax
import jax.numpy as jnp
from jax import lax
from jax.experimental import pallas as pl
from jax.experimental.pallas import tpu as pltpu
from jax.sharding import PartitionSpec as P

NX, NY, NZ, NC, NR = 4, 4, 2, 2, 4
SIDE = 128
CLS = 172
CP = 176
GROWS = 1280
F32 = jnp.float32
VMEM = pl.BlockSpec(memory_space=pltpu.VMEM)
SMEM = pl.BlockSpec(memory_space=pltpu.SMEM)
ANY = pl.BlockSpec(memory_space=pl.ANY)
MIB = 1024 * 1024
COUNTS, ME, REP = 32, 36, 37


def row_perm(shift):
    pairs = []
    for x in range(NX):
        for y in range(NY):
            for z in range(NZ):
                for c in range(NC):
                    dx, dy, dz, dc = shift(c)
                    src = ((x * NY + y) * NZ + z) * NC + c
                    dst = (((x + dx) % NX * NY + (y + dy) % NY) * NZ + (z ^ dz)) * NC + (c ^ dc)
                    pairs.append((src, dst))
    return pairs


def send_core(a):
    return lax.ppermute(a, "row", row_perm(lambda c: (0, 0, 0, 1)))


def send_z(a):
    return lax.ppermute(a, "row", row_perm(lambda c: (0, 0, 1, 0)))


def send_plane(a, stage, d):
    return lax.ppermute(
        a, "row", row_perm(lambda c: (d, 0, 0, 0) if c == stage else (0, d, 0, 0))
    )


def send_rep(a, d):
    return lax.ppermute(a, "rep", [(j, (j + d) % NR) for j in range(NR)])


def swap_rep(a, bit):
    return lax.ppermute(a, "rep", [(j, j ^ bit) for j in range(NR)])


def split(a):
    hi = a.astype(jnp.bfloat16)
    lo = (a - hi.astype(F32)).astype(jnp.bfloat16)
    return hi, lo


def dot3(a, b, dims=((1,), (0,))):
    dn = (dims, ((), ()))
    ah, al = split(a)
    bh, bl = split(b)
    mm = lambda p, q: lax.dot_general(p, q, dn, preferred_element_type=F32)
    return mm(ah, bh) + (mm(ah, bl) + mm(al, bh))


def wide(a):
    return jnp.concatenate(split(a), axis=1)


def twice(a):
    w = wide(a)
    return jnp.concatenate([w, w], axis=0)


def twice_t(w):
    h, l = w[:, :SIDE], w[:, SIDE:]
    return jnp.concatenate(
        [jnp.concatenate([h, h], axis=1), jnp.concatenate([l, l], axis=1)], axis=0
    )


def fold(a):
    return a[:, :SIDE] + a[:, SIDE:]


def relative(c, me):
    diff = c ^ me
    dx = ((c >> 4) - (me >> 4)) & 3
    dy = ((c >> 2) - (me >> 2)) & 3
    core = c & 1
    d1 = jnp.where(core == 0, dx, dy)
    d2 = jnp.where(core == 0, dy, dx)
    return d1, d2, (diff >> 1) & 1, diff & 1


def stage_kernel(meta, tiles, out):
    for block in range(4):
        for k in range(8):
            t = tiles[block, 0, k]
            out[block, k] = wide(jnp.where(k < meta[COUNTS + block], t, jnp.zeros_like(t)))


def load_pieces(refs, buf, sems):
    copies = []
    start = 0
    for k, ref in enumerate(refs):
        size = ref.shape[0]
        copies.append(pltpu.make_async_copy(ref, buf.at[pl.ds(start, size)], sems.at[k]))
        start += size
    for c in copies:
        c.start()
    for c in copies:
        c.wait()


def agg_kernel(second, meta, tiles, *rest):
    refs, outs, (buf, sems) = rest[:6], rest[6:8], rest[8:]
    me, rep = meta[ME], meta[REP]
    load_pieces(refs, buf, sems)
    rows = buf.shape[1]
    for d in range(NR):
        block = rep ^ d

        def step(i, acc, block=block):
            for u in range(2):
                s = 2 * i + u
                d1, d2, dz, dc = relative(meta[block * 8 + s], me)
                piece = buf[((dc * 4 + d2) * 4 + d1) * 2 + dz]
                tile = tiles[block, s]
                if second:
                    dn = (((1,), (1,)), ((), ()))
                    acc += lax.dot_general(
                        wide(piece), twice_t(tile), dn, preferred_element_type=F32
                    )
                else:
                    acc += jnp.dot(tile, twice(piece), preferred_element_type=F32)
            return acc

        pairs = (meta[COUNTS + block] + 1) >> 1
        outs[d & 1][d >> 1] = fold(lax.fori_loop(0, pairs, step, jnp.zeros((rows, 256), F32)))


def transposed_kernel(meta, tiles, near, far, own, oth, ct_buf):
    me, rep = meta[ME], meta[REP]
    for o in (own, oth):
        o[...] = jnp.zeros(o.shape, F32)
    for d in range(NR):
        block = rep ^ d
        ct_buf[...] = jnp.concatenate(
            [wide((near, far)[d & 1][d >> 1]), jnp.zeros((CP - CLS, 256), jnp.bfloat16)], axis=0
        )

        def step(i, _, block=block):
            done = []
            for u in range(2):
                s = 2 * i + u
                tile = jnp.concatenate([tiles[block, s]] * 2, axis=0)
                done.append((s, fold(jnp.dot(ct_buf[...], tile, preferred_element_type=F32))))
            for s, r in done:
                d1, d2, dz, dc = relative(meta[block * 8 + s], me)
                at = (d1 * 4 + d2) * 2 + dz

                @pl.when(dc == 0)
                def _():
                    own[at] += r

                @pl.when(dc != 0)
                def _():
                    oth[at] += r

            return 0

        lax.fori_loop(0, (meta[COUNTS + block] + 1) >> 1, step, 0)


def hidden_kernel(kept, got, last, feat, self_one, neigh_one, bias, nt, agg, pre, yt):
    total = (kept[0] + got[0]) + last[...]
    agg[...] = total
    p = dot3(feat[...], self_one[...]) + dot3(total, neigh_one[...]) + bias[...]
    pre[...] = p
    h = p * jax.nn.sigmoid(p)
    yt[pl.ds(CP - 8, 8)] = jnp.zeros((8, SIDE), F32)
    yt[pl.ds(0, CLS)] = dot3(nt[...], h, ((1,), (1,)))


def grad_kernel(meta, g, gz, pre, agg, feat, ct, st, nt, bias_two, base, same, other, packed):
    p = pre[...]
    s = jax.nn.sigmoid(p)
    h = p * s
    base[...] = dot3(st[...], h, ((1,), (1,))) + jnp.broadcast_to(bias_two[...], (SIDE, CLS)).T
    gt = g[pl.ds(0, CLS)] + gz[pl.ds(0, CLS)]
    cot = ct[...].T
    gh = dot3(cot, st[...]) + dot3(gt.T, nt[...])
    gp = gh * s * (1.0 + p * (1.0 - s))
    bias_one_grad = jnp.sum(gp, axis=0, keepdims=True)
    bias_two_grad = jnp.sum(cot, axis=0, keepdims=True)

    def put(start, value):
        rows = value.shape[0]
        packed[pl.ds(start, rows)] = value[:, :SIDE]
        packed[pl.ds(608 + start, rows)] = value[:, SIDE:]

    for start in (424, 600, 1032, 1208):
        packed[pl.ds(start, 8)] = jnp.zeros((8, SIDE), F32)
    packed[pl.ds(1216, 64)] = jnp.zeros((64, SIDE), F32)
    put(0, dot3(feat[...].T, gp))
    put(128, dot3(agg[...].T, gp))
    put(256, dot3(ct[...], h))
    put(432, dot3(gt, h))
    packed[pl.ds(256 + CLS, 1)] = bias_one_grad[:, :SIDE]
    packed[pl.ds(608 + 256 + CLS, 1)] = bias_one_grad[:, SIDE:]
    packed[pl.ds(432 + CLS, 1)] = bias_two_grad[:, :SIDE]
    packed[pl.ds(608 + 432 + CLS, 1), : CLS - SIDE] = bias_two_grad[:, SIDE:]
    for slot, d, start in piece_order(meta):
        (same, other)[slot][d] = packed[pl.ds(start, 160)]


def piece_order(meta):
    me = meta[ME]
    for slot in range(2):
        core = (me & 1) ^ slot
        at = jnp.where(core == 0, me >> 4, me >> 2)
        for d in range(4):
            start = (core * 4 + ((at + d) & 3)) * 160
            yield slot, d, pl.multiple_of(start, 8)


def finish_kernel(meta, q, qo, gs1, gn1, gb1, gs2, gn2, gb2, packed):
    for slot, d, start in piece_order(meta):
        packed[pl.ds(start, 160)] = (q, qo)[slot][d]

    def take(start, rows):
        return jnp.concatenate(
            [packed[pl.ds(start, rows)], packed[pl.ds(608 + start, rows)]], axis=1
        )

    gs1[...] = take(0, 128)
    gn1[...] = take(128, 128)
    gs2[...] = take(256, CLS)
    gn2[...] = take(432, CLS)
    gb1[...] = take(256 + CLS, 1)
    gb2[...] = take(432 + CLS, 1)[:, :CLS]


def logits_kernel(kept, got, last, base, out):
    part = pl.ds(0, CLS)
    out[...] = base[...] + ((kept[0, part] + got[0, part]) + last[part])


def call(kernel, outs, ins, scratch=(), smem=0, in_any=(), mib=8, cost=6, dtype=F32):
    specs = [SMEM] * smem + [VMEM] * (len(ins) - smem)
    for k in in_any:
        specs[k] = ANY
    return pl.pallas_call(
        kernel,
        out_shape=[jax.ShapeDtypeStruct(s, dtype) for s in outs],
        in_specs=specs,
        out_specs=[VMEM] * len(outs),
        scratch_shapes=list(scratch),
        cost_estimate=pl.CostEstimate(flops=0, bytes_accessed=cost * MIB, transcendentals=0),
        compiler_params=pltpu.CompilerParams(vmem_limit_bytes=mib * MIB),
    )(*ins)


def after(a, *others):
    return lax.optimization_barrier((a, *others))[0]


def add4(a, b, c, d):
    return (a + b) + (c + d)


def gather_lane(block, swapped, *held):
    pair = after(jnp.stack([block, swapped]), *held)
    return jnp.concatenate([pair] + [send_plane(pair, 0, -d) for d in (1, 2, 3)])


def gather_plane(lane):
    return [lane] + [send_plane(lane, 1, -d) for d in (1, 2, 3)]


def gather_ring(lane):
    one, three = send_plane(lane, 1, 3), send_plane(lane, 1, 1)
    two = jnp.concatenate([send_plane(one[:4], 1, 3), send_plane(three[4:], 1, 1)])
    return [lane, one, two, three]


def gather_core(plane, *held):
    rest = jnp.concatenate([after(plane[1], *held)] + plane[2:])
    return plane + [send_core(plane[0]), send_core(rest)]


def scatter_core(own, oth):
    got = send_core(oth)
    return [own[8 * d : 8 * d + 8] + got[8 * d : 8 * d + 8] for d in range(4)]


def scatter_lane(parts, *held):
    one, three = send_plane(parts[1], 0, 1), send_plane(parts[3], 0, 3)
    return [parts[0], one, send_plane(after(parts[2], *held), 0, 2), three]


def scatter_plane(q):
    q = add4(q[:2], *(send_plane(q[2 * d : 2 * d + 2], 1, d) for d in (1, 2, 3)))
    return q[0], send_z(q[1])


def reduce_lane(same, other):
    got = send_core(other)
    parts = [same[d] + got[d] for d in range(4)]
    return add4(parts[0], *(send_plane(parts[d], 0, d) for d in (1, 2, 3)))


def last_sums(q, products):
    kept, given = products
    got = swap_rep(given, 1)
    last = swap_rep(kept[1] + got[1], 2)
    q = after(q, kept) + send_z(q)
    q = add4(q, *(send_plane(q, 1, d) for d in (1, 2, 3)))
    q = after(q, got)
    q = jnp.stack([q] + [send_plane(q, 0, -d) for d in (1, 2, 3)])
    q = after(q, last)
    return kept, got, last, q, send_core(q)


def agg(second, head, pieces):
    rows = pieces[0].shape[1]
    shape = (rows, SIDE)
    return call(
        functools.partial(agg_kernel, second), [(2,) + shape] * 2, head + tuple(pieces),
        scratch=(
            pltpu.VMEM((64, rows, SIDE), F32),
            pltpu.SemaphoreType.DMA((6,)),
        ),
        smem=1, in_any=range(2, 8), mib=16, cost=12,
    )


def shards(
    features,
    tiles,
    columns,
    counts,
    self_one,
    neigh_one,
    bias_one,
    self_two,
    neigh_two,
    bias_two,
    cotangent,
):
    place = jnp.stack([lax.axis_index("row"), lax.axis_index("rep")]).astype(jnp.int32)
    meta = jnp.concatenate([columns.reshape(-1), counts.reshape(-1), place])
    (staged,) = call(
        stage_kernel, [(4, 8, SIDE, 256)], (meta, tiles), smem=1, dtype=jnp.bfloat16
    )
    head = (meta, staged)
    block = (SIDE, SIDE)
    tall, padded = (CLS, SIDE), (CP, SIDE)
    ct, st, nt = cotangent.T, self_two.T, neigh_two.T

    swapped = send_z(features)
    pair = jnp.stack([ct, swap_rep(ct, 2)])
    far = swap_rep(pair, 1)
    lane = gather_lane(features, swapped, staged)
    own, oth = call(
        transposed_kernel, [(32,) + padded] * 2, head + (after(pair, lane), far),
        scratch=(pltpu.VMEM((CP, 256), jnp.bfloat16),), smem=1, mib=16, cost=12,
    )
    plane = gather_plane(lane)
    parts = scatter_core(own, oth)
    laned = scatter_lane(parts, *plane[1:])
    pieces = gather_core(plane, *parts)
    products = agg(False, head, pieces)

    kept, given = products
    got = swap_rep(given, 1)
    last = swap_rep(kept[1] + got[1], 2)
    q = add4(after(laned[0], got), *laned[1:])
    sums, pre, yt = call(
        hidden_kernel, [block, (SIDE, 256), padded],
        (kept, got, last, features, self_one, neigh_one, bias_one.reshape(1, -1), nt),
    )
    g, gz = scatter_plane(q)
    lane = gather_lane(yt, send_z(yt))
    base, same, other = call(
        grad_kernel, [tall, (4, 160, SIDE), (4, 160, SIDE)],
        (meta, g, gz, after(pre, lane), sums, features, ct, st, nt, bias_two.reshape(1, -1)),
        scratch=(pltpu.VMEM((GROWS, SIDE), F32),), smem=1,
    )
    plane = gather_ring(after(lane, gz))
    kept = reduce_lane(same, other)
    kept = kept + swap_rep(kept, 1)
    pieces = gather_core(plane, kept)
    kept = kept + swap_rep(kept, 2)
    pieces[-1] = after(pieces[-1], kept)
    products = agg(True, head, pieces)
    *parts, q, qo = last_sums(kept, products)
    (logits,) = call(logits_kernel, [tall], (*parts, base))
    gs1, gn1, gb1, gs2, gn2, gb2 = call(
        finish_kernel,
        [(128, 256), (128, 256), (1, 256), (CLS, 256), (CLS, 256), (1, CLS)],
        (meta, q, qo), scratch=(pltpu.VMEM((GROWS, SIDE), F32),), smem=1,
    )
    return logits.T, gs1, gn1, gb1.reshape(-1), gs2.T, gn2.T, gb2.reshape(-1)


def solution(mesh):
    return jax.shard_map(
        shards,
        mesh=mesh,
        in_specs=(
            P(("row", "rep"), None),
            P("row", "rep", None, None, None),
            P("row", "rep", None),
            P("row", "rep"),
            P(),
            P(),
            P(),
            P(),
            P(),
            P(),
            P(("row", "rep"), None),
        ),
        out_specs=(P(("row", "rep"), None), P(), P(), P(), P(), P(), P()),
        check_vma=False,
    )
```

```python
import functools

import jax
import jax.numpy as jnp
from jax import lax
from jax.experimental import pallas as pl
from jax.experimental.pallas import tpu as pltpu
from jax.sharding import PartitionSpec as P

NX, NY, NZ, NC, NR = 4, 4, 2, 2, 4
SIDE = 128
CLS = 172
CP = 176
GROWS = 1280
F32 = jnp.float32
VMEM = pl.BlockSpec(memory_space=pltpu.VMEM)
SMEM = pl.BlockSpec(memory_space=pltpu.SMEM)
ANY = pl.BlockSpec(memory_space=pl.ANY)
MIB = 1024 * 1024
COUNTS, ME, REP = 32, 36, 37


def row_perm(shift):
    pairs = []
    for x in range(NX):
        for y in range(NY):
            for z in range(NZ):
                for c in range(NC):
                    dx, dy, dz, dc = shift(c)
                    src = ((x * NY + y) * NZ + z) * NC + c
                    dst = (((x + dx) % NX * NY + (y + dy) % NY) * NZ + (z ^ dz)) * NC + (c ^ dc)
                    pairs.append((src, dst))
    return pairs


def send_core(a):
    return lax.ppermute(a, "row", row_perm(lambda c: (0, 0, 0, 1)))


def send_z(a):
    return lax.ppermute(a, "row", row_perm(lambda c: (0, 0, 1, 0)))


def send_plane(a, stage, d):
    return lax.ppermute(
        a, "row", row_perm(lambda c: (d, 0, 0, 0) if c == stage else (0, d, 0, 0))
    )


def send_rep(a, d):
    return lax.ppermute(a, "rep", [(j, (j + d) % NR) for j in range(NR)])


def swap_rep(a, bit):
    return lax.ppermute(a, "rep", [(j, j ^ bit) for j in range(NR)])


def split(a):
    hi = a.astype(jnp.bfloat16)
    lo = (a - hi.astype(F32)).astype(jnp.bfloat16)
    return hi, lo


def dot3(a, b, dims=((1,), (0,))):
    dn = (dims, ((), ()))
    ah, al = split(a)
    bh, bl = split(b)
    mm = lambda p, q: lax.dot_general(p, q, dn, preferred_element_type=F32)
    return mm(ah, bh) + (mm(ah, bl) + mm(al, bh))


def wide(a):
    return jnp.concatenate(split(a), axis=1)


def twice(a):
    w = wide(a)
    return jnp.concatenate([w, w], axis=0)


def twice_t(w):
    h, l = w[:, :SIDE], w[:, SIDE:]
    return jnp.concatenate(
        [jnp.concatenate([h, h], axis=1), jnp.concatenate([l, l], axis=1)], axis=0
    )


def fold(a):
    return a[:, :SIDE] + a[:, SIDE:]


def relative(c, me):
    diff = c ^ me
    dx = ((c >> 4) - (me >> 4)) & 3
    dy = ((c >> 2) - (me >> 2)) & 3
    core = c & 1
    d1 = jnp.where(core == 0, dx, dy)
    d2 = jnp.where(core == 0, dy, dx)
    return d1, d2, (diff >> 1) & 1, diff & 1


def stage_kernel(meta, tiles, out):
    for block in range(4):
        for k in range(8):
            t = tiles[block, 0, k]
            out[block, k] = wide(jnp.where(k < meta[COUNTS + block], t, jnp.zeros_like(t)))


def load_pieces(refs, buf, sems):
    copies = []
    start = 0
    for k, ref in enumerate(refs):
        size = ref.shape[0]
        copies.append(pltpu.make_async_copy(ref, buf.at[pl.ds(start, size)], sems.at[k]))
        start += size
    for c in copies:
        c.start()
    for c in copies:
        c.wait()


def agg_kernel(second, meta, tiles, *rest):
    refs, outs, (buf, sems) = rest[:6], rest[6:8], rest[8:]
    me, rep = meta[ME], meta[REP]
    load_pieces(refs, buf, sems)
    rows = buf.shape[1]
    for d in range(NR):
        block = rep ^ d

        def step(i, acc, block=block):
            for u in range(2):
                s = 2 * i + u
                d1, d2, dz, dc = relative(meta[block * 8 + s], me)
                piece = buf[((dc * 4 + d2) * 4 + d1) * 2 + dz]
                tile = tiles[block, s]
                if second:
                    dn = (((1,), (1,)), ((), ()))
                    acc += lax.dot_general(
                        wide(piece), twice_t(tile), dn, preferred_element_type=F32
                    )
                else:
                    acc += jnp.dot(tile, twice(piece), preferred_element_type=F32)
            return acc

        pairs = (meta[COUNTS + block] + 1) >> 1
        outs[d & 1][d >> 1] = fold(lax.fori_loop(0, pairs, step, jnp.zeros((rows, 256), F32)))


def transposed_kernel(meta, tiles, near, far, own, oth, ct_buf):
    me, rep = meta[ME], meta[REP]
    for o in (own, oth):
        o[...] = jnp.zeros(o.shape, F32)
    for d in range(NR):
        block = rep ^ d
        ct_buf[...] = jnp.concatenate(
            [wide((near, far)[d & 1][d >> 1]), jnp.zeros((CP - CLS, 256), jnp.bfloat16)], axis=0
        )

        def step(i, _, block=block):
            done = []
            for u in range(2):
                s = 2 * i + u
                tile = jnp.concatenate([tiles[block, s]] * 2, axis=0)
                done.append((s, fold(jnp.dot(ct_buf[...], tile, preferred_element_type=F32))))
            for s, r in done:
                d1, d2, dz, dc = relative(meta[block * 8 + s], me)
                at = (d1 * 4 + d2) * 2 + dz

                @pl.when(dc == 0)
                def _():
                    own[at] += r

                @pl.when(dc != 0)
                def _():
                    oth[at] += r

            return 0

        lax.fori_loop(0, (meta[COUNTS + block] + 1) >> 1, step, 0)


def hidden_kernel(kept, got, last, feat, self_one, neigh_one, bias, nt, agg, pre, yt):
    total = (kept[0] + got[0]) + last[...]
    agg[...] = total
    p = dot3(feat[...], self_one[...]) + dot3(total, neigh_one[...]) + bias[...]
    pre[...] = p
    h = p * jax.nn.sigmoid(p)
    yt[pl.ds(CP - 8, 8)] = jnp.zeros((8, SIDE), F32)
    yt[pl.ds(0, CLS)] = dot3(nt[...], h, ((1,), (1,)))


def grad_kernel(meta, g, gz, pre, agg, feat, ct, st, nt, bias_two, base, same, other, packed):
    p = pre[...]
    s = jax.nn.sigmoid(p)
    h = p * s
    base[...] = dot3(st[...], h, ((1,), (1,))) + jnp.broadcast_to(bias_two[...], (SIDE, CLS)).T
    gt = g[pl.ds(0, CLS)] + gz[pl.ds(0, CLS)]
    cot = ct[...].T
    gh = dot3(cot, st[...]) + dot3(gt.T, nt[...])
    gp = gh * s * (1.0 + p * (1.0 - s))
    bias_one_grad = jnp.sum(gp, axis=0, keepdims=True)
    bias_two_grad = jnp.sum(cot, axis=0, keepdims=True)

    def put(start, value):
        rows = value.shape[0]
        packed[pl.ds(start, rows)] = value[:, :SIDE]
        packed[pl.ds(608 + start, rows)] = value[:, SIDE:]

    for start in (424, 600, 1032, 1208):
        packed[pl.ds(start, 8)] = jnp.zeros((8, SIDE), F32)
    packed[pl.ds(1216, 64)] = jnp.zeros((64, SIDE), F32)
    put(0, dot3(feat[...].T, gp))
    put(128, dot3(agg[...].T, gp))
    put(256, dot3(ct[...], h))
    put(432, dot3(gt, h))
    packed[pl.ds(256 + CLS, 1)] = bias_one_grad[:, :SIDE]
    packed[pl.ds(608 + 256 + CLS, 1)] = bias_one_grad[:, SIDE:]
    packed[pl.ds(432 + CLS, 1)] = bias_two_grad[:, :SIDE]
    packed[pl.ds(608 + 432 + CLS, 1), : CLS - SIDE] = bias_two_grad[:, SIDE:]
    for slot, d, start in piece_order(meta):
        (same, other)[slot][d] = packed[pl.ds(start, 160)]


def piece_order(meta):
    me = meta[ME]
    for slot in range(2):
        core = (me & 1) ^ slot
        at = jnp.where(core == 0, me >> 4, me >> 2)
        for d in range(4):
            start = (core * 4 + ((at + d) & 3)) * 160
            yield slot, d, pl.multiple_of(start, 8)


def finish_kernel(meta, q, qo, gs1, gn1, gb1, gs2, gn2, gb2, packed):
    for slot, d, start in piece_order(meta):
        packed[pl.ds(start, 160)] = (q, qo)[slot][d]

    def take(start, rows):
        return jnp.concatenate(
            [packed[pl.ds(start, rows)], packed[pl.ds(608 + start, rows)]], axis=1
        )

    gs1[...] = take(0, 128)
    gn1[...] = take(128, 128)
    gs2[...] = take(256, CLS)
    gn2[...] = take(432, CLS)
    gb1[...] = take(256 + CLS, 1)
    gb2[...] = take(432 + CLS, 1)[:, :CLS]


def logits_kernel(kept, got, last, base, out):
    part = pl.ds(0, CLS)
    out[...] = base[...] + ((kept[0, part] + got[0, part]) + last[part])


def call(kernel, outs, ins, scratch=(), smem=0, in_any=(), mib=8, cost=6, dtype=F32):
    specs = [SMEM] * smem + [VMEM] * (len(ins) - smem)
    for k in in_any:
        specs[k] = ANY
    return pl.pallas_call(
        kernel,
        out_shape=[jax.ShapeDtypeStruct(s, dtype) for s in outs],
        in_specs=specs,
        out_specs=[VMEM] * len(outs),
        scratch_shapes=list(scratch),
        cost_estimate=pl.CostEstimate(flops=0, bytes_accessed=cost * MIB, transcendentals=0),
        compiler_params=pltpu.CompilerParams(vmem_limit_bytes=mib * MIB),
    )(*ins)


def after(a, *others):
    return lax.optimization_barrier((a, *others))[0]


def add4(a, b, c, d):
    return (a + b) + (c + d)


def gather_lane(block, swapped, *held):
    pair = after(jnp.stack([block, swapped]), *held)
    return jnp.concatenate([pair] + [send_plane(pair, 0, -d) for d in (1, 2, 3)])


def gather_plane(lane):
    return [lane] + [send_plane(lane, 1, -d) for d in (1, 2, 3)]


def gather_ring(lane):
    one, three = send_plane(lane, 1, 3), send_plane(lane, 1, 1)
    two = jnp.concatenate([send_plane(one[:4], 1, 3), send_plane(three[4:], 1, 1)])
    return [lane, one, two, three]


def gather_core(plane, *held):
    rest = jnp.concatenate([after(plane[1], *held)] + plane[2:])
    return plane + [send_core(plane[0]), send_core(rest)]


def scatter_core(own, oth):
    got = send_core(oth)
    return [own[8 * d : 8 * d + 8] + got[8 * d : 8 * d + 8] for d in range(4)]


def scatter_lane(parts, *held):
    one, three = send_plane(parts[1], 0, 1), send_plane(parts[3], 0, 3)
    return [parts[0], one, send_plane(after(parts[2], *held), 0, 2), three]


def scatter_plane(q):
    q = add4(q[:2], *(send_plane(q[2 * d : 2 * d + 2], 1, d) for d in (1, 2, 3)))
    return q[0], send_z(q[1])


def reduce_lane(same, other):
    got = send_core(other)
    parts = [same[d] + got[d] for d in range(4)]
    return add4(parts[0], *(send_plane(parts[d], 0, d) for d in (1, 2, 3)))


def last_sums(q, products):
    kept, given = products
    got = swap_rep(given, 1)
    last = swap_rep(kept[1] + got[1], 2)
    q = after(q, kept) + send_z(q)
    q = add4(q, *(send_plane(q, 1, d) for d in (1, 2, 3)))
    q = after(q, got)
    q = jnp.stack([q] + [send_plane(q, 0, -d) for d in (1, 2, 3)])
    q = after(q, last)
    return kept, got, last, q, send_core(q)


def agg(second, head, pieces):
    rows = pieces[0].shape[1]
    shape = (rows, SIDE)
    return call(
        functools.partial(agg_kernel, second), [(2,) + shape] * 2, head + tuple(pieces),
        scratch=(
            pltpu.VMEM((64, rows, SIDE), F32),
            pltpu.SemaphoreType.DMA((6,)),
        ),
        smem=1, in_any=range(2, 8), mib=16, cost=12,
    )


def shards(
    features,
    tiles,
    columns,
    counts,
    self_one,
    neigh_one,
    bias_one,
    self_two,
    neigh_two,
    bias_two,
    cotangent,
):
    place = jnp.stack([lax.axis_index("row"), lax.axis_index("rep")]).astype(jnp.int32)
    meta = jnp.concatenate([columns.reshape(-1), counts.reshape(-1), place])
    (staged,) = call(
        stage_kernel, [(4, 8, SIDE, 256)], (meta, tiles), smem=1, dtype=jnp.bfloat16
    )
    head = (meta, staged)
    block = (SIDE, SIDE)
    tall, padded = (CLS, SIDE), (CP, SIDE)
    ct, st, nt = cotangent.T, self_two.T, neigh_two.T

    swapped = send_z(features)
    pair = jnp.stack([ct, swap_rep(ct, 2)])
    far = swap_rep(pair, 1)
    lane = gather_lane(features, swapped, staged)
    own, oth = call(
        transposed_kernel, [(32,) + padded] * 2, head + (after(pair, lane), far),
        scratch=(pltpu.VMEM((CP, 256), jnp.bfloat16),), smem=1, mib=16, cost=12,
    )
    plane = gather_plane(lane)
    parts = scatter_core(own, oth)
    laned = scatter_lane(parts, *plane[1:])
    pieces = gather_core(plane, *parts)
    products = agg(False, head, pieces)

    kept, given = products
    got = swap_rep(given, 1)
    last = swap_rep(kept[1] + got[1], 2)
    q = add4(after(laned[0], last), *laned[1:])
    sums, pre, yt = call(
        hidden_kernel, [block, (SIDE, 256), padded],
        (kept, got, last, features, self_one, neigh_one, bias_one.reshape(1, -1), nt),
    )
    g, gz = scatter_plane(q)
    lane = gather_lane(yt, send_z(yt))
    base, same, other = call(
        grad_kernel, [tall, (4, 160, SIDE), (4, 160, SIDE)],
        (meta, g, gz, after(pre, lane), sums, features, ct, st, nt, bias_two.reshape(1, -1)),
        scratch=(pltpu.VMEM((GROWS, SIDE), F32),), smem=1,
    )
    plane = gather_ring(after(lane, gz))
    kept = reduce_lane(same, other)
    kept = kept + swap_rep(kept, 1)
    kept = kept + swap_rep(kept, 2)
    pieces = gather_core(plane, kept)
    products = agg(True, head, pieces)
    *parts, q, qo = last_sums(kept, products)
    (logits,) = call(logits_kernel, [tall], (*parts, base))
    gs1, gn1, gb1, gs2, gn2, gb2 = call(
        finish_kernel,
        [(128, 256), (128, 256), (1, 256), (CLS, 256), (CLS, 256), (1, CLS)],
        (meta, q, qo), scratch=(pltpu.VMEM((GROWS, SIDE), F32),), smem=1,
    )
    return logits.T, gs1, gn1, gb1.reshape(-1), gs2.T, gn2.T, gb2.reshape(-1)


def solution(mesh):
    return jax.shard_map(
        shards,
        mesh=mesh,
        in_specs=(
            P(("row", "rep"), None),
            P("row", "rep", None, None, None),
            P("row", "rep", None),
            P("row", "rep"),
            P(),
            P(),
            P(),
            P(),
            P(),
            P(),
            P(("row", "rep"), None),
        ),
        out_specs=(P(("row", "rep"), None), P(), P(), P(), P(), P(), P()),
        check_vma=False,
    )
```

```python
import functools

import jax
import jax.numpy as jnp
from jax import lax
from jax.experimental import pallas as pl
from jax.experimental.pallas import tpu as pltpu
from jax.sharding import PartitionSpec as P

NX, NY, NZ, NC, NR = 4, 4, 2, 2, 4
SIDE = 128
CLS = 172
CP = 176
GROWS = 1280
F32 = jnp.float32
VMEM = pl.BlockSpec(memory_space=pltpu.VMEM)
SMEM = pl.BlockSpec(memory_space=pltpu.SMEM)
ANY = pl.BlockSpec(memory_space=pl.ANY)
MIB = 1024 * 1024
COUNTS, ME, REP = 32, 36, 37


def row_perm(shift):
    pairs = []
    for x in range(NX):
        for y in range(NY):
            for z in range(NZ):
                for c in range(NC):
                    dx, dy, dz, dc = shift(c)
                    src = ((x * NY + y) * NZ + z) * NC + c
                    dst = (((x + dx) % NX * NY + (y + dy) % NY) * NZ + (z ^ dz)) * NC + (c ^ dc)
                    pairs.append((src, dst))
    return pairs


def send_core(a):
    return lax.ppermute(a, "row", row_perm(lambda c: (0, 0, 0, 1)))


def send_z(a):
    return lax.ppermute(a, "row", row_perm(lambda c: (0, 0, 1, 0)))


def send_plane(a, stage, d):
    return lax.ppermute(
        a, "row", row_perm(lambda c: (d, 0, 0, 0) if c == stage else (0, d, 0, 0))
    )


def send_rep(a, d):
    return lax.ppermute(a, "rep", [(j, (j + d) % NR) for j in range(NR)])


def swap_rep(a, bit):
    return lax.ppermute(a, "rep", [(j, j ^ bit) for j in range(NR)])


def split(a):
    hi = a.astype(jnp.bfloat16)
    lo = (a - hi.astype(F32)).astype(jnp.bfloat16)
    return hi, lo


def dot3(a, b, dims=((1,), (0,))):
    dn = (dims, ((), ()))
    ah, al = split(a)
    bh, bl = split(b)
    mm = lambda p, q: lax.dot_general(p, q, dn, preferred_element_type=F32)
    return mm(ah, bh) + (mm(ah, bl) + mm(al, bh))


def wide(a):
    return jnp.concatenate(split(a), axis=1)


def twice(a):
    w = wide(a)
    return jnp.concatenate([w, w], axis=0)


def twice_t(w):
    h, l = w[:, :SIDE], w[:, SIDE:]
    return jnp.concatenate(
        [jnp.concatenate([h, h], axis=1), jnp.concatenate([l, l], axis=1)], axis=0
    )


def fold(a):
    return a[:, :SIDE] + a[:, SIDE:]


def relative(c, me):
    diff = c ^ me
    dx = ((c >> 4) - (me >> 4)) & 3
    dy = ((c >> 2) - (me >> 2)) & 3
    core = c & 1
    d1 = jnp.where(core == 0, dx, dy)
    d2 = jnp.where(core == 0, dy, dx)
    return d1, d2, (diff >> 1) & 1, diff & 1


def stage_kernel(meta, tiles, out):
    for block in range(4):
        for k in range(8):
            t = tiles[block, 0, k]
            out[block, k] = wide(jnp.where(k < meta[COUNTS + block], t, jnp.zeros_like(t)))


def load_pieces(refs, buf, sems):
    copies = []
    start = 0
    for k, ref in enumerate(refs):
        size = ref.shape[0]
        copies.append(pltpu.make_async_copy(ref, buf.at[pl.ds(start, size)], sems.at[k]))
        start += size
    for c in copies:
        c.start()
    for c in copies:
        c.wait()


def agg_kernel(second, meta, tiles, *rest):
    refs, outs, (buf, sems) = rest[:6], rest[6:8], rest[8:]
    me, rep = meta[ME], meta[REP]
    load_pieces(refs, buf, sems)
    rows = buf.shape[1]
    for d in range(NR):
        block = rep ^ d

        def step(i, acc, block=block):
            for u in range(2):
                s = 2 * i + u
                d1, d2, dz, dc = relative(meta[block * 8 + s], me)
                piece = buf[((dc * 4 + d2) * 4 + d1) * 2 + dz]
                tile = tiles[block, s]
                if second:
                    dn = (((1,), (1,)), ((), ()))
                    acc += lax.dot_general(
                        wide(piece), twice_t(tile), dn, preferred_element_type=F32
                    )
                else:
                    acc += jnp.dot(tile, twice(piece), preferred_element_type=F32)
            return acc

        pairs = (meta[COUNTS + block] + 1) >> 1
        outs[d & 1][d >> 1] = fold(lax.fori_loop(0, pairs, step, jnp.zeros((rows, 256), F32)))


def transposed_kernel(meta, tiles, near, far, own, oth, ct_buf):
    me, rep = meta[ME], meta[REP]
    for o in (own, oth):
        o[...] = jnp.zeros(o.shape, F32)
    for d in range(NR):
        block = rep ^ d
        ct_buf[...] = jnp.concatenate(
            [wide((near, far)[d & 1][d >> 1]), jnp.zeros((CP - CLS, 256), jnp.bfloat16)], axis=0
        )

        def step(i, _, block=block):
            done = []
            for u in range(2):
                s = 2 * i + u
                tile = jnp.concatenate([tiles[block, s]] * 2, axis=0)
                done.append((s, fold(jnp.dot(ct_buf[...], tile, preferred_element_type=F32))))
            for s, r in done:
                d1, d2, dz, dc = relative(meta[block * 8 + s], me)
                at = (d1 * 4 + d2) * 2 + dz

                @pl.when(dc == 0)
                def _():
                    own[at] += r

                @pl.when(dc != 0)
                def _():
                    oth[at] += r

            return 0

        lax.fori_loop(0, (meta[COUNTS + block] + 1) >> 1, step, 0)


def hidden_kernel(kept, got, last, feat, self_one, neigh_one, bias, nt, agg, pre, yt):
    total = (kept[0] + got[0]) + last[...]
    agg[...] = total
    p = dot3(feat[...], self_one[...]) + dot3(total, neigh_one[...]) + bias[...]
    pre[...] = p
    h = p * jax.nn.sigmoid(p)
    yt[pl.ds(CP - 8, 8)] = jnp.zeros((8, SIDE), F32)
    yt[pl.ds(0, CLS)] = dot3(nt[...], h, ((1,), (1,)))


def grad_kernel(meta, g, gz, pre, agg, feat, ct, st, nt, bias_two, base, same, other, packed):
    p = pre[...]
    s = jax.nn.sigmoid(p)
    h = p * s
    base[...] = dot3(st[...], h, ((1,), (1,))) + jnp.broadcast_to(bias_two[...], (SIDE, CLS)).T
    gt = g[pl.ds(0, CLS)] + gz[pl.ds(0, CLS)]
    cot = ct[...].T
    gh = dot3(cot, st[...]) + dot3(gt.T, nt[...])
    gp = gh * s * (1.0 + p * (1.0 - s))
    bias_one_grad = jnp.sum(gp, axis=0, keepdims=True)
    bias_two_grad = jnp.sum(cot, axis=0, keepdims=True)

    def put(start, value):
        rows = value.shape[0]
        packed[pl.ds(start, rows)] = value[:, :SIDE]
        packed[pl.ds(608 + start, rows)] = value[:, SIDE:]

    for start in (424, 600, 1032, 1208):
        packed[pl.ds(start, 8)] = jnp.zeros((8, SIDE), F32)
    packed[pl.ds(1216, 64)] = jnp.zeros((64, SIDE), F32)
    put(0, dot3(feat[...].T, gp))
    put(128, dot3(agg[...].T, gp))
    put(256, dot3(ct[...], h))
    put(432, dot3(gt, h))
    packed[pl.ds(256 + CLS, 1)] = bias_one_grad[:, :SIDE]
    packed[pl.ds(608 + 256 + CLS, 1)] = bias_one_grad[:, SIDE:]
    packed[pl.ds(432 + CLS, 1)] = bias_two_grad[:, :SIDE]
    packed[pl.ds(608 + 432 + CLS, 1), : CLS - SIDE] = bias_two_grad[:, SIDE:]
    for slot, d, start in piece_order(meta):
        (same, other)[slot][d] = packed[pl.ds(start, 160)]


def piece_order(meta):
    me = meta[ME]
    for slot in range(2):
        core = (me & 1) ^ slot
        at = jnp.where(core == 0, me >> 4, me >> 2)
        for d in range(4):
            start = (core * 4 + ((at + d) & 3)) * 160
            yield slot, d, pl.multiple_of(start, 8)


def finish_kernel(meta, q, qo, gs1, gn1, gb1, gs2, gn2, gb2, packed):
    for slot, d, start in piece_order(meta):
        packed[pl.ds(start, 160)] = (q, qo)[slot][d]

    def take(start, rows):
        return jnp.concatenate(
            [packed[pl.ds(start, rows)], packed[pl.ds(608 + start, rows)]], axis=1
        )

    gs1[...] = take(0, 128)
    gn1[...] = take(128, 128)
    gs2[...] = take(256, CLS)
    gn2[...] = take(432, CLS)
    gb1[...] = take(256 + CLS, 1)
    gb2[...] = take(432 + CLS, 1)[:, :CLS]


def logits_kernel(kept, got, last, base, out):
    part = pl.ds(0, CLS)
    out[...] = base[...] + ((kept[0, part] + got[0, part]) + last[part])


def call(kernel, outs, ins, scratch=(), smem=0, in_any=(), mib=8, cost=6, dtype=F32):
    specs = [SMEM] * smem + [VMEM] * (len(ins) - smem)
    for k in in_any:
        specs[k] = ANY
    return pl.pallas_call(
        kernel,
        out_shape=[jax.ShapeDtypeStruct(s, dtype) for s in outs],
        in_specs=specs,
        out_specs=[VMEM] * len(outs),
        scratch_shapes=list(scratch),
        cost_estimate=pl.CostEstimate(flops=0, bytes_accessed=cost * MIB, transcendentals=0),
        compiler_params=pltpu.CompilerParams(vmem_limit_bytes=mib * MIB),
    )(*ins)


def after(a, *others):
    return lax.optimization_barrier((a, *others))[0]


def add4(a, b, c, d):
    return (a + b) + (c + d)


def gather_lane(block, swapped, *held):
    pair = after(jnp.stack([block, swapped]), *held)
    return jnp.concatenate([pair] + [send_plane(pair, 0, -d) for d in (1, 2, 3)])


def gather_plane(lane):
    return [lane] + [send_plane(lane, 1, -d) for d in (1, 2, 3)]


def gather_ring(lane):
    one, three = send_plane(lane, 1, 3), send_plane(lane, 1, 1)
    two = jnp.concatenate([send_plane(one[:4], 1, 3), send_plane(three[4:], 1, 1)])
    return [lane, one, two, three]


def gather_core(plane, *held):
    rest = jnp.concatenate([after(plane[1], *held)] + plane[2:])
    return plane + [send_core(plane[0]), send_core(rest)]


def scatter_core(own, oth):
    got = send_core(oth)
    return [own[8 * d : 8 * d + 8] + got[8 * d : 8 * d + 8] for d in range(4)]


def scatter_lane(parts, *held):
    one, three = send_plane(parts[1], 0, 1), send_plane(parts[3], 0, 3)
    return [parts[0], one, send_plane(after(parts[2], *held), 0, 2), three]


def scatter_plane(q):
    q = add4(q[:2], *(send_plane(q[2 * d : 2 * d + 2], 1, d) for d in (1, 2, 3)))
    return q


def reduce_lane(same, other):
    got = send_core(other)
    parts = [same[d] + got[d] for d in range(4)]
    return add4(parts[0], *(send_plane(parts[d], 0, d) for d in (1, 2, 3)))


def last_sums(q, products):
    kept, given = products
    got = swap_rep(given, 1)
    last = swap_rep(kept[1] + got[1], 2)
    q = after(q, kept) + send_z(q)
    q = add4(q, *(send_plane(q, 1, d) for d in (1, 2, 3)))
    q = after(q, got)
    q = jnp.stack([q] + [send_plane(q, 0, -d) for d in (1, 2, 3)])
    q = after(q, last)
    return kept, got, last, q, send_core(q)


def agg(second, head, pieces):
    rows = pieces[0].shape[1]
    shape = (rows, SIDE)
    return call(
        functools.partial(agg_kernel, second), [(2,) + shape] * 2, head + tuple(pieces),
        scratch=(
            pltpu.VMEM((64, rows, SIDE), F32),
            pltpu.SemaphoreType.DMA((6,)),
        ),
        smem=1, in_any=range(2, 8), mib=16, cost=12,
    )


def shards(
    features,
    tiles,
    columns,
    counts,
    self_one,
    neigh_one,
    bias_one,
    self_two,
    neigh_two,
    bias_two,
    cotangent,
):
    place = jnp.stack([lax.axis_index("row"), lax.axis_index("rep")]).astype(jnp.int32)
    meta = jnp.concatenate([columns.reshape(-1), counts.reshape(-1), place])
    (staged,) = call(
        stage_kernel, [(4, 8, SIDE, 256)], (meta, tiles), smem=1, dtype=jnp.bfloat16
    )
    head = (meta, staged)
    block = (SIDE, SIDE)
    tall, padded = (CLS, SIDE), (CP, SIDE)
    ct, st, nt = cotangent.T, self_two.T, neigh_two.T

    swapped = send_z(features)
    pair = jnp.stack([ct, swap_rep(ct, 2)])
    far = swap_rep(pair, 1)
    lane = gather_lane(features, swapped, staged)
    own, oth = call(
        transposed_kernel, [(32,) + padded] * 2, head + (after(pair, lane), far),
        scratch=(pltpu.VMEM((CP, 256), jnp.bfloat16),), smem=1, mib=16, cost=12,
    )
    plane = gather_plane(lane)
    parts = scatter_core(own, oth)
    laned = scatter_lane(parts, *plane[1:])
    pieces = gather_core(plane, *parts)
    products = agg(False, head, pieces)

    kept, given = products
    got = swap_rep(given, 1)
    last = swap_rep(kept[1] + got[1], 2)
    q = add4(after(laned[0], last), *laned[1:])
    sums, pre, yt = call(
        hidden_kernel, [block, (SIDE, 256), padded],
        (kept, got, last, features, self_one, neigh_one, bias_one.reshape(1, -1), nt),
    )
    q_two = scatter_plane(q)
    g, gz = q_two[0], send_z(q_two[1])
    lane = gather_lane(yt, send_z(yt))
    base, same, other = call(
        grad_kernel, [tall, (4, 160, SIDE), (4, 160, SIDE)],
        (meta, g, gz, after(pre, lane), sums, features, ct, st, nt, bias_two.reshape(1, -1)),
        scratch=(pltpu.VMEM((GROWS, SIDE), F32),), smem=1,
    )
    plane = gather_ring(after(lane, q_two))
    kept = reduce_lane(same, other)
    kept = kept + swap_rep(kept, 1)
    kept = kept + swap_rep(kept, 2)
    pieces = gather_core(plane, kept)
    products = agg(True, head, pieces)
    *parts, q, qo = last_sums(kept, products)
    (logits,) = call(logits_kernel, [tall], (*parts, base))
    gs1, gn1, gb1, gs2, gn2, gb2 = call(
        finish_kernel,
        [(128, 256), (128, 256), (1, 256), (CLS, 256), (CLS, 256), (1, CLS)],
        (meta, q, qo), scratch=(pltpu.VMEM((GROWS, SIDE), F32),), smem=1,
    )
    return logits.T, gs1, gn1, gb1.reshape(-1), gs2.T, gn2.T, gb2.reshape(-1)


def solution(mesh):
    return jax.shard_map(
        shards,
        mesh=mesh,
        in_specs=(
            P(("row", "rep"), None),
            P("row", "rep", None, None, None),
            P("row", "rep", None),
            P("row", "rep"),
            P(),
            P(),
            P(),
            P(),
            P(),
            P(),
            P(("row", "rep"), None),
        ),
        out_specs=(P(("row", "rep"), None), P(), P(), P(), P(), P(), P()),
        check_vma=False,
    )
```
